32 devices in a mesh: section: 2 (over x), ctx: 16 (over z, y, core).
Axes of the slice: x: 2, y: 2, z: 4, core: 2. Of those that a mesh axis runs over, the one named last changes fastest.
Arguments:
- query_rows: bfloat16 [2, 2048, 1536], P('section', 'ctx'), may hold values from -5 to 5
- key_rows: bfloat16 [2, 2048, 1536], P('section', 'ctx'), may hold values from -5 to 5
- value_rows: bfloat16 [2, 2048, 1536], P('section', 'ctx'), may hold values from -6 to 6
- grad_output: bfloat16 [2, 2048, 1536], P('section', 'ctx'), may hold values from -6 to 6
- block_lists: int32 [16, 5], P('ctx'), may hold values from -1 to 15, as said below
Outputs:
- grad_query: bfloat16 [2, 2048, 1536], P('section', 'ctx')
- grad_key: bfloat16 [2, 2048, 1536], P('section', 'ctx')
- grad_value: bfloat16 [2, 2048, 1536], P('section', 'ctx')
- handoff: bfloat16 [2, 2048, 1536], P('section', 'ctx')
The draws below stay inside these ranges and needn't reach their ends.
Inputs may be any that keep to these rules, and one draw needn't show every extreme that they name: `block_lists`: each list names distinct key blocks whose devices lie within 2 devices of the query block's device, always including the query block itself; -1 marks an unused entry; in every draw some query block names all 5 blocks.
All inputs are finite; a program needn't handle non-finite values.
Results may differ from the reference program's by a relative error of at most 0.011.
Values may be sent and summed in bfloat16 or wider, within the bound.
No kernel may reach another device: no remote copies, remote signals or barrier semaphores. Data moves between devices by JAX's collectives and lax.ppermute only.
A program may use at most 128 MiB of HBM per device.

```python
import jax
import jax.numpy as jnp
from jax import lax

H = 12
DH = 128
BLK = 128
BPD = 1
REACH = 2
HD = 1536
NBLK = 16
SEQ = 2048
MAXN = 5
SECTIONS = 2


def query_key_pair(key):
    shape = (SECTIONS, NBLK, BLK, HD)
    first = jax.random.fold_in(key, 701)
    second = jax.random.fold_in(key, 702)
    queries = jnp.clip(jax.random.normal(first, shape, jnp.float32), -4.5, 4.5)
    keys_all = jnp.clip(jax.random.normal(second, shape, jnp.float32), -4.5, 4.5)
    return (queries.reshape(SECTIONS, SEQ, HD), keys_all.reshape(SECTIONS, SEQ, HD))


def draw_query_rows(key, part):
    return query_key_pair(key)[0].astype(jnp.bfloat16)


def draw_key_rows(key, part):
    return query_key_pair(key)[1].astype(jnp.bfloat16)


def draw_block_lists(key, part):
    devices_all = NBLK // BPD
    query_block = jnp.arange(NBLK).reshape(NBLK, 1)
    query_device = query_block // BPD
    column = jnp.arange(MAXN).reshape(1, MAXN)
    distance = column // BPD - REACH
    within = column % BPD
    candidate = (query_device + distance) * BPD + within
    inside = (candidate >= 0) & (candidate < NBLK)
    rolled = jax.random.randint(jax.random.fold_in(key, 801), (NBLK, MAXN), 0, 100)
    keep = rolled < 100 - 15 * jnp.abs(distance)
    full_device = jax.random.randint(jax.random.fold_in(key, 802), (), REACH, devices_all - REACH)
    full_block = full_device * BPD + jax.random.randint(jax.random.fold_in(key, 803), (), 0, BPD)
    keep = keep | (candidate == query_block) | (query_block == full_block)
    return jnp.where(inside & keep, candidate, -1).astype(jnp.int32)


def shard_levels(key, shape, pieces, low, largest):
    level = 1.0
    for dim, blocks in pieces:
        heights = jax.random.uniform(jax.random.fold_in(jax.random.fold_in(key, 6), dim), (blocks,), jnp.float32, low / len(pieces), largest / len(pieces))
        level = level * jnp.repeat(jnp.exp(heights), shape[dim] // blocks).reshape((-1,) + (1,) * (len(shape) - 1 - dim))
    return level


def scatter_about(rng, shape, scale, bound, split=(), dtype=jnp.bfloat16):
    loudness = shard_levels(rng, shape, split, -0.22, 0.18) if split else 1.0
    result = jax.random.normal(rng, shape, jnp.float32) * scale * loudness
    return jnp.minimum(jnp.maximum(result, -bound), bound).astype(dtype)


def setup_inputs(seed: int = 0) -> dict:
    streams_of = jax.random.split(jax.random.key(seed), 6)
    return {
        "query_rows": draw_query_rows(jax.random.fold_in(streams_of[5], 71), 0),
        "key_rows": draw_key_rows(jax.random.fold_in(streams_of[5], 71), 0),
        "value_rows": scatter_about(streams_of[2], (SECTIONS, SEQ, HD), 1.0, 6.0, ((0, 2), (1, 16))),
        "grad_output": scatter_about(streams_of[3], (SECTIONS, SEQ, HD), 1.0, 6.0, ((0, 2), (1, 16))),
        "block_lists": draw_block_lists(jax.random.fold_in(streams_of[5], 71), 0),
    }


big_negative = -1.0e30


def layer_grads(query_rows, key_rows, value_rows, grad_output, block_lists):
    scale = DH ** -0.5
    blocks = block_lists.shape[0]
    query_blocks = query_rows.reshape(blocks, BLK, H, DH)
    key_blocks = key_rows.reshape(blocks, BLK, H, DH)
    value_blocks = value_rows.reshape(blocks, BLK, H, DH)
    grad_blocks = grad_output.reshape(blocks, BLK, H, DH)

    def visit(carry, inputs):
        key_acc, value_acc = carry
        query_one, grad_one, listed = inputs
        usable = listed >= 0
        picked = jnp.maximum(listed, 0).astype(jnp.int32)
        keys_here = key_blocks[picked].astype(jnp.float32)
        values_here = value_blocks[picked].astype(jnp.float32)
        query_full = query_one.astype(jnp.float32)
        grad_full = grad_one.astype(jnp.float32)
        scores = jnp.einsum("qhd,nkhd->hqnk", query_full, keys_here) * scale
        scores = jnp.where(usable[None, None, :, None], scores, big_negative)
        highest = jnp.max(scores, axis=(2, 3), keepdims=True)
        weights = jnp.exp(scores - highest)
        probs = weights / jnp.sum(weights, axis=(2, 3), keepdims=True)
        probs_back = lax.optimization_barrier(probs.astype(jnp.bfloat16)).astype(jnp.float32)
        attended = jnp.einsum("hqnk,nkhd->qhd", probs_back, values_here)
        delta = jnp.sum(grad_full * attended, axis=2)
        value_part = jnp.einsum("hqnk,qhd->nkhd", probs_back, grad_full)
        grad_probs = jnp.einsum("qhd,nkhd->hqnk", grad_full, values_here)
        grad_scores = probs * (grad_probs - jnp.transpose(delta)[:, :, None, None])
        scores_back = lax.optimization_barrier(grad_scores.astype(jnp.bfloat16)).astype(jnp.float32)
        query_part = jnp.einsum("hqnk,nkhd->qhd", scores_back, keys_here) * scale
        key_part = jnp.einsum("hqnk,qhd->nkhd", scores_back, query_full) * scale
        key_acc = key_acc.at[picked].add(key_part)
        value_acc = value_acc.at[picked].add(value_part)
        return (key_acc, value_acc), query_part

    empty = jnp.zeros((blocks, BLK, H, DH), jnp.float32)
    (key_acc, value_acc), query_grads = lax.scan(visit, (empty, empty), (query_blocks, grad_blocks, block_lists))
    total = blocks * BLK
    width = H * DH
    return (query_grads.reshape(total, width).astype(jnp.bfloat16),
            key_acc.reshape(total, width).astype(jnp.bfloat16),
            value_acc.reshape(total, width).astype(jnp.bfloat16))


def reference(query_rows, key_rows, value_rows, grad_output, block_lists):
    query_list = []
    key_list = []
    value_list = []
    for layer in range(SECTIONS):
        grad_q, grad_k, grad_v = layer_grads(query_rows[layer], key_rows[layer], value_rows[layer], grad_output[layer], block_lists)
        query_list.append(grad_q)
        key_list.append(grad_k)
        value_list.append(grad_v)
    grad_query = jnp.stack(query_list)
    grad_key = jnp.stack(key_list)
    grad_value = jnp.stack(value_list)
    handoff = jnp.concatenate([grad_value[1:], jnp.zeros_like(grad_value[:1])], axis=0)
    return grad_query, grad_key, grad_value, handoff
```

```python
import jax
import jax.numpy as jnp
from jax import lax
from jax.experimental import pallas as pl
from jax.experimental.pallas import tpu as pltpu
from jax.sharding import PartitionSpec as P

H = 12
DH = 128
BLK = 128
REACH = 2
TEAM = 4
LOCAL = H // TEAM
SPAN = 2 * REACH + 1
SLOTS = TEAM + 2 * REACH
SCALE = DH ** (-0.5)
LOG2E = 1.4426950408889634
OFF = -1e30
MASK = 16

bf16 = jnp.bfloat16
f32 = jnp.float32


def member():
    return lax.rem(lax.axis_index("ctx"), TEAM)


def rows_of(index, count=BLK):
    return pl.ds(pl.multiple_of(index * BLK, BLK), count)


def pack_kernel(lists, q, k, v, g, own, one, kv2, kv3, qg2, qg3, edge):
    block = lax.axis_index("ctx")
    me = member()
    row = lax.broadcasted_iota(jnp.int32, (MASK, DH), 0)
    mask = jnp.full((MASK, DH), OFF, f32)
    for o in range(SPAN):
        wanted = jnp.int32(0)
        for n in range(lists.shape[1]):
            entry = lists[0, n]
            hit = (entry >= 0) & (entry == block + (o - REACH))
            wanted = jnp.maximum(wanted, hit.astype(jnp.int32))
        level = jnp.where(wanted > 0, 0.0, OFF).astype(f32)
        mask = jnp.where(row == o, level, mask)
    mask = mask.astype(bf16)

    def cut(source, group, h):
        start = pl.multiple_of(group * (LOCAL * DH) + h * DH, DH)
        return source[0, :, pl.ds(start, DH)]

    for h in range(LOCAL):
        for target, step in ((own, 0), (one, 1)):
            group = jnp.bitwise_xor(me, step)
            for n, source in enumerate((k, v, q, g)):
                piece = cut(source, group, h)
                target[h, n * BLK : (n + 1) * BLK, :] = piece
                if n < 2:
                    edge[step, h, n * BLK : (n + 1) * BLK, :] = piece
            target[h, 4 * BLK :, :] = mask
        for kv, qg, step in ((kv2, qg2, 2), (kv3, qg3, 3)):
            group = jnp.bitwise_xor(me, step)
            for n, source in enumerate((k, v)):
                kv[h, n * BLK : (n + 1) * BLK, :] = cut(source, group, h)
            for n, source in enumerate((q, g)):
                qg[h, n * BLK : (n + 1) * BLK, :] = cut(source, group, h)
            qg[h, 2 * BLK :, :] = mask


def nt(a, b):
    return lax.dot_general(a, b, (((1,), (1,)), ((), ())), preferred_element_type=f32)


def tn(a, b):
    return lax.dot_general(a, b, (((0,), (0,)), ((), ())), preferred_element_type=f32)


def nn(a, b):
    return lax.dot_general(a, b, (((1,), (0,)), ((), ())), preferred_element_type=f32)


def attend_kernel(
    own, one, kv2, kv3, qg2, qg3, edge0, edge1, late2, late3,
    dq0, dq1, dq2, dq3, dv_own, dk_own, dv_low, dv_high, dk_low, dk_high,
    ks, vs, qs, gs, bs, ps, ss, dqs,
):
    me = member()
    side = me // 2
    core = lax.rem(me, 2)
    other = 1 - core

    def put_kv(slot, source, lead=0):
        ks[rows_of(slot), :] = source[(0,) * lead + (slice(0, BLK),)]
        vs[rows_of(slot), :] = source[(0,) * lead + (slice(BLK, 2 * BLK),)]

    def put_qg(position, source, base):
        qs[rows_of(position), :] = source[0, base : base + BLK]
        gs[rows_of(position), :] = source[0, base + BLK : base + 2 * BLK]
        bs[pl.ds(pl.multiple_of(position * MASK, MASK), MASK), :] = source[
            0, base + 2 * BLK : base + 2 * BLK + MASK
        ]

    for step, source in ((0, own), (1, one), (2, kv2), (3, kv3)):
        put_kv(REACH + jnp.bitwise_xor(me, step), source, 1)
    for step, source, base in ((0, own, 2 * BLK), (1, one, 2 * BLK), (2, qg2, 0), (3, qg3, 0)):
        put_qg(jnp.bitwise_xor(me, step), source, base)
    near = (1 - side) * (REACH + TEAM)
    far = side * (REACH + TEAM)
    put_kv(near + core, edge0, 2)
    put_kv(near + other, edge1, 2)
    put_kv(far + core, late2, 1)
    put_kv(far + other, late3, 1)

    for i in range(TEAM):
        here = slice(i * BLK, (i + 1) * BLK)
        reach = slice(i * BLK, (i + SPAN) * BLK)
        keys, values = ks[reach, :], vs[reach, :]
        query, grad = qs[here, :], gs[here, :]
        bias = bs[i * MASK : (i + 1) * MASK, :].astype(f32)
        scores = nt(keys, query) * (SCALE * LOG2E)
        scores = jnp.concatenate(
            [scores[o * BLK : (o + 1) * BLK] + bias[o : o + 1] for o in range(SPAN)], axis=0
        )
        highest = jnp.max(scores, axis=0, keepdims=True)
        weights = jnp.exp2(scores - highest)
        probs = weights * (1.0 / jnp.sum(weights, axis=0, keepdims=True))
        probs_low = probs.astype(bf16)
        grad_probs = nt(values, grad)
        delta = jnp.sum(probs_low.astype(f32) * grad_probs, axis=0, keepdims=True)
        scores_low = (probs * (grad_probs - delta)).astype(bf16)
        dqs[here, :] = (tn(scores_low, keys) * SCALE).astype(bf16)
        ps[reach, here] = probs_low
        ss[reach, here] = scores_low
    for step, target in enumerate((dq0, dq1, dq2, dq3)):
        target[0] = dqs[rows_of(jnp.bitwise_xor(me, step)), :]
    for j in range(SLOTS):
        there = slice(j * BLK, (j + 1) * BLK)
        seen = slice(max(0, j - SPAN + 1) * BLK, (min(TEAM - 1, j) + 1) * BLK)
        dv = nn(ps[there, seen], gs[seen, :])
        dk = nn(ss[there, seen], qs[seen, :]) * SCALE
        if j < REACH:
            dv_low[0, there, :] = dv.astype(bf16)
            dk_low[0, there, :] = dk.astype(bf16)
        elif j < REACH + TEAM:
            at = slice((j - REACH) * BLK, (j - REACH + 1) * BLK)
            dv_own[0, at, :] = dv
            dk_own[0, at, :] = dk
        else:
            at = slice((j - REACH - TEAM) * BLK, (j - REACH - TEAM + 1) * BLK)
            dv_high[0, at, :] = dv.astype(bf16)
            dk_high[0, at, :] = dk.astype(bf16)


def total_kernel(mine, from_below, from_above, out0, out1, out2, out3):
    me = member()
    half = REACH * BLK
    for step, target in enumerate((out0, out1, out2, out3)):
        block = jnp.bitwise_xor(me, step)
        low = block < REACH
        at = rows_of(lax.rem(block, REACH))
        term = jnp.where(low, from_below[0, at, :].astype(f32), from_above[0, at, :].astype(f32))
        target[0] = (mine[0, rows_of(block), :] + term).astype(bf16)


def unpack_kernel(in0, in1, in2, in3, out):
    me = member()
    for step, source in enumerate((in0, in1, in2, in3)):
        group = jnp.bitwise_xor(me, step)
        for h in range(LOCAL):
            start = pl.multiple_of(group * (LOCAL * DH) + h * DH, DH)
            out[0, :, pl.ds(start, DH)] = source[h]


def struct(*shape, dtype=bf16):
    return jax.ShapeDtypeStruct(shape, dtype)


VM = pl.BlockSpec(memory_space=pltpu.VMEM)


def per_head(*tail):
    return pl.BlockSpec((1, *tail), lambda h: (h, 0, 0))


def params():
    return pltpu.CompilerParams(vmem_limit_bytes=40 * 1024 * 1024)


def shards(query_rows, key_rows, value_rows, grad_output, block_lists):
    ctx = lax.axis_size("ctx")
    width = query_rows.shape[2]

    def swap(array, step):
        return lax.ppermute(array, "ctx", [(i, i ^ step) for i in range(ctx)])

    def ring(array, low, high):
        pairs = [
            (i, (i + TEAM * (low if i % TEAM < TEAM // 2 else high)) % ctx) for i in range(ctx)
        ]
        return lax.ppermute(array, "ctx", pairs)

    kv = struct(LOCAL, 2 * BLK, DH)
    qg = struct(LOCAL, 2 * BLK + MASK, DH)
    full = struct(LOCAL, 4 * BLK + MASK, DH)
    own, one, kv2, kv3, qg2, qg3, edge = pl.pallas_call(
        pack_kernel,
        out_shape=(full, full, kv, kv, qg, qg, struct(2, LOCAL, 2 * BLK, DH)),
        in_specs=[pl.BlockSpec(memory_space=pltpu.SMEM)] + [VM] * 4,
        out_specs=[VM] * 7,
        compiler_params=params(),
        name="pack",
    )(block_lists, query_rows, key_rows, value_rows, grad_output)

    kv2 = swap(kv2, 2)
    kv3 = swap(kv3, 3)
    edge0 = ring(edge, -1, 1)
    one = swap(one, 1)
    qg2 = swap(qg2, 2)
    qg3 = swap(qg3, 3)
    edge1 = swap(edge0, 1)
    late2 = ring(kv2, 1, -1)
    late3 = ring(kv3, 1, -1)

    block = struct(LOCAL, BLK, DH)
    kept = struct(LOCAL, TEAM * BLK, DH, dtype=f32)
    halo = struct(LOCAL, REACH * BLK, DH)
    piece = per_head(BLK, DH)
    (dq0, dq1, dq2, dq3, dv_own, dk_own, dv_low, dv_high, dk_low, dk_high) = pl.pallas_call(
        attend_kernel,
        grid=(LOCAL,),
        out_shape=(block,) * 4 + (kept,) * 2 + (halo,) * 4,
        in_specs=[per_head(4 * BLK + MASK, DH)] * 2
        + [per_head(2 * BLK, DH)] * 2
        + [per_head(2 * BLK + MASK, DH)] * 2
        + [
            pl.BlockSpec((1, 1, 2 * BLK, DH), lambda h: (0, h, 0, 0)),
            pl.BlockSpec((1, 1, 2 * BLK, DH), lambda h: (1, h, 0, 0)),
        ]
        + [per_head(2 * BLK, DH)] * 2,
        out_specs=[piece] * 4 + [per_head(TEAM * BLK, DH)] * 2 + [per_head(REACH * BLK, DH)] * 4,
        scratch_shapes=[
            pltpu.VMEM((SLOTS * BLK, DH), bf16),
            pltpu.VMEM((SLOTS * BLK, DH), bf16),
            pltpu.VMEM((TEAM * BLK, DH), bf16),
            pltpu.VMEM((TEAM * BLK, DH), bf16),
            pltpu.VMEM((TEAM * MASK, DH), bf16),
            pltpu.VMEM((SLOTS * BLK, TEAM * BLK), bf16),
            pltpu.VMEM((SLOTS * BLK, TEAM * BLK), bf16),
            pltpu.VMEM((TEAM * BLK, DH), bf16),
        ],
        compiler_params=params(),
        name="attend",
    )(own, one, kv2, kv3, qg2, qg3, edge0, edge1, late2, late3)

    def total(mine, low, high):
        below = ring(high, 1, 1)
        above = ring(low, -1, -1)
        return pl.pallas_call(
            total_kernel,
            grid=(LOCAL,),
            out_shape=(block,) * 4,
            in_specs=[per_head(TEAM * BLK, DH)] + [per_head(REACH * BLK, DH)] * 2,
            out_specs=[piece] * 4,
            compiler_params=params(),
            name="total",
        )(mine, below, above)

    def home(parts):
        parts = [parts[0]] + [swap(parts[step], step) for step in range(1, TEAM)]
        return pl.pallas_call(
            unpack_kernel,
            out_shape=struct(1, BLK, width),
            in_specs=[VM] * 4,
            out_specs=VM,
            compiler_params=params(),
            name="unpack",
        )(*parts)

    grad_value = home(total(dv_own, dv_low, dv_high))
    sections = lax.axis_size("section")
    handoff = lax.ppermute(grad_value, "section", [(s + 1, s) for s in range(sections - 1)])
    grad_query = home((dq0, dq1, dq2, dq3))
    grad_key = home(total(dk_own, dk_low, dk_high))
    return (grad_query, grad_key, grad_value, handoff)


def solution(mesh):
    wide = P("section", "ctx", None)
    return jax.shard_map(
        shards,
        mesh=mesh,
        in_specs=(wide, wide, wide, wide, P("ctx", None)),
        out_specs=(wide,) * 4,
        check_vma=False,
    )
```

```python
import functools

import jax
import jax.numpy as jnp
from jax import lax
from jax.experimental import pallas as pl
from jax.experimental.pallas import tpu as pltpu
from jax.sharding import PartitionSpec as P

H = 12
DH = 128
BLK = 128
REACH = 2
TEAM = 4
LOCAL = H // TEAM
SPAN = 2 * REACH + 1
SLOTS = TEAM + 2 * REACH
SCALE = DH ** (-0.5)
LOG2E = 1.4426950408889634
OFF = -1e30
MASK = 16
QG = 2 * BLK + MASK

bf16 = jnp.bfloat16
f32 = jnp.float32


def member():
    return lax.rem(lax.axis_index("ctx"), TEAM)


def rows_of(index, count=BLK):
    return pl.ds(pl.multiple_of(index * BLK, BLK), count)


def head_columns(group, h):
    return pl.ds(pl.multiple_of(group * (LOCAL * DH) + h * DH, DH), DH)


def pieces(source, target, sems):
    count = sems.shape[0]
    rows = BLK // count
    return [
        pltpu.make_async_copy(
            source.at[0, n * rows : (n + 1) * rows], target.at[0, n * rows : (n + 1) * rows], sems.at[n]
        )
        for n in range(count)
    ]


def cut(source, targets):
    me = member()
    for step, (target, base) in enumerate(targets):
        group = jnp.bitwise_xor(me, step)
        for h in range(LOCAL):
            target[h, base : base + BLK, :] = source[0, :, head_columns(group, h)]


def keys_kernel(k_hbm, k0, k1, k2, k3, k, sems):
    copies = pieces(k_hbm, k, sems)
    for copy in copies:
        copy.start()
    for copy in copies:
        copy.wait()
    cut(k, ((k0, 0), (k1, 0), (k2, 0), (k3, 0)))


def rest_kernel(
    v_hbm, q_hbm, g_hbm, lists_hbm, v0, qg0, one, v2, v3, qg2, qg3, lists, lists_sem, v, q, g, sems
):
    copies = [
        pieces(source, target, sems.at[n])
        for n, (source, target) in enumerate(((v_hbm, v), (q_hbm, q), (g_hbm, g)))
    ]
    lists_copy = pltpu.make_async_copy(lists_hbm, lists, lists_sem)
    lists_copy.start()
    for group in copies:
        for copy in group:
            copy.start()
    block = lax.axis_index("ctx")
    lists_copy.wait()
    row = lax.broadcasted_iota(jnp.int32, (MASK, DH), 0)
    mask = jnp.full((MASK, DH), OFF, f32)
    for o in range(SPAN):
        wanted = jnp.int32(0)
        for n in range(lists.shape[1]):
            entry = lists[0, n]
            hit = (entry >= 0) & (entry == block + (o - REACH))
            wanted = jnp.maximum(wanted, hit.astype(jnp.int32))
        level = jnp.where(wanted > 0, 0.0, OFF).astype(f32)
        mask = jnp.where(row == o, level, mask)
    mask = mask.astype(bf16)
    for target in (qg0, one, qg2, qg3):
        for h in range(LOCAL):
            target[h, 2 * BLK : QG, :] = mask
    targets = (
        ((v0, 0), (one, QG), (v2, 0), (v3, 0)),
        ((qg0, 0), (one, 0), (qg2, 0), (qg3, 0)),
        ((qg0, BLK), (one, BLK), (qg2, BLK), (qg3, BLK)),
    )
    for group, source, places in zip(copies, (v, q, g), targets):
        for copy in group:
            copy.wait()
        cut(source, places)


def merge_kernel(first, second, both):
    both[0] = first[...]
    both[1] = second[...]


def stage_kernel(base, zero, one, two, three, local, first, second):
    me = member()
    core = lax.rem(me, 2)
    for h in range(LOCAL):
        local[h, rows_of(me), :] = zero[h]
        local[h, rows_of(jnp.bitwise_xor(me, 1)), :] = one[h, base : base + BLK]
        local[h, rows_of(jnp.bitwise_xor(me, 2)), :] = two[h]
        local[h, rows_of(jnp.bitwise_xor(me, 3)), :] = three[h]
    for h in range(LOCAL):
        first[h] = local[h, rows_of(REACH * (1 - core), REACH * BLK), :]
        second[h] = local[h, rows_of(REACH * core, REACH * BLK), :]


def nt(a, b):
    return lax.dot_general(a, b, (((1,), (1,)), ((), ())), preferred_element_type=f32)


def tn(a, b):
    return lax.dot_general(a, b, (((0,), (0,)), ((), ())), preferred_element_type=f32)


def nn(a, b):
    return lax.dot_general(a, b, (((1,), (0,)), ((), ())), preferred_element_type=f32)


def line_up(slots, h, local, first, second):
    core = lax.rem(member(), 2)
    top = REACH + TEAM
    slots[h, REACH * BLK : top * BLK, :] = local[h]
    slots[h, rows_of(core * top, REACH * BLK), :] = first[h]
    slots[h, rows_of((1 - core) * top, REACH * BLK), :] = second[h]


def key_sums(weights, rows, h, mine, ends, scale):
    for j in range(SLOTS):
        there = slice(j * BLK, (j + 1) * BLK)
        seen = slice(max(0, j - SPAN + 1) * BLK, (min(TEAM - 1, j) + 1) * BLK)
        term = nn(weights[h, there, seen], rows[h, seen, :])
        if scale is not None:
            term = term * scale
        if REACH <= j < REACH + TEAM:
            mine[h, (j - REACH) * BLK : (j - REACH + 1) * BLK, :] = term
        else:
            at = j if j < REACH else j - TEAM
            ends[at * BLK : (at + 1) * BLK, :] = term.astype(bf16)


def hand_ends(h, ends, first, second):
    core = lax.rem(member(), 2)
    first[h] = ends[rows_of(REACH * (1 - core), REACH * BLK), :]
    second[h] = ends[rows_of(REACH * core, REACH * BLK), :]


def probs_kernel(
    qg0, one, qg23, local, halo1, halo2, probs, ks, qs, gs, dv_own, dv1, dv2, bs, ends
):
    me = member()
    for h in range(LOCAL):
        line_up(ks, h, local, halo1, halo2)
        for step, source in enumerate((qg0, one, qg23.at[0], qg23.at[1])):
            position = jnp.bitwise_xor(me, step)
            qs[h, rows_of(position), :] = source[h, :BLK]
            gs[h, rows_of(position), :] = source[h, BLK : 2 * BLK]
            if h == 0:
                at = pl.ds(pl.multiple_of(position * MASK, MASK), MASK)
                bs[at, :] = source[h, 2 * BLK : QG]
    for h in range(LOCAL):
        for pair in range(TEAM // 2):
            first = 2 * pair
            keys = ks[h, first * BLK : (first + SPAN + 1) * BLK, :]
            query = qs[h, first * BLK : (first + 2) * BLK, :]
            both = nt(keys, query)
            for n in range(2):
                i = first + n
                here = slice(i * BLK, (i + 1) * BLK)
                reach = slice(i * BLK, (i + SPAN) * BLK)
                bias = bs[i * MASK : (i + 1) * MASK, :].astype(f32)
                lanes = slice(n * BLK, (n + 1) * BLK)
                scores = jnp.concatenate(
                    [
                        both[(n + o) * BLK : (n + o + 1) * BLK, lanes] * (SCALE * LOG2E)
                        + bias[o : o + 1]
                        for o in range(SPAN)
                    ],
                    axis=0,
                )
                highest = jnp.max(scores, axis=0, keepdims=True)
                weights = jnp.exp2(scores - highest)
                scaled = weights * (1.0 / jnp.sum(weights, axis=0, keepdims=True))
                probs[h, reach, here] = scaled.astype(bf16)
        key_sums(probs, gs, h, dv_own, ends, None)
        hand_ends(h, ends, dv1, dv2)


def grads_kernel(
    probs, ks, qs, gs, local, halo1, halo2, dq0, dq1, dq23, dk_own, dk1, dk2, vs, ss, dqs, ends
):
    me = member()
    for h in range(LOCAL):
        line_up(vs, h, local, halo1, halo2)
        for pair in range(TEAM // 2):
            first = 2 * pair
            values = vs[h, first * BLK : (first + SPAN + 1) * BLK, :]
            grad = gs[h, first * BLK : (first + 2) * BLK, :]
            both = nt(values, grad)
            for n in range(2):
                i = first + n
                here = slice(i * BLK, (i + 1) * BLK)
                reach = slice(i * BLK, (i + SPAN) * BLK)
                grad_probs = both[n * BLK : (n + SPAN) * BLK, n * BLK : (n + 1) * BLK]
                weights = probs[h, reach, here].astype(f32)
                delta = jnp.sum(weights * grad_probs, axis=0, keepdims=True)
                scores_low = (weights * (grad_probs - delta)).astype(bf16)
                ss[h, reach, here] = scores_low
                dqs[here, :] = (tn(scores_low, ks[h, reach, :]) * SCALE).astype(bf16)
        for step, target in enumerate((dq0, dq1, dq23.at[0], dq23.at[1])):
            target[h] = dqs[rows_of(jnp.bitwise_xor(me, step)), :]
        key_sums(ss, qs, h, dk_own, ends, SCALE)
        hand_ends(h, ends, dk1, dk2)


def total_kernel(mine, ring1, ring2, out0, out1, out2, out3):
    me = member()
    core = lax.rem(me, 2)
    for step, target in enumerate((out0, out1, out2, out3)):
        block = jnp.bitwise_xor(me, step)
        use1 = block // REACH == core
        at = rows_of(lax.rem(block, REACH))
        for h in range(LOCAL):
            term = jnp.where(use1, ring1[h, at, :].astype(f32), ring2[h, at, :].astype(f32))
            target[h] = (mine[h, rows_of(block), :] + term).astype(bf16)


def unpack_kernel(in0, in1, in2, in3, out_hbm, out, sems):
    me = member()
    for step, source in enumerate((in0, in1, in2, in3)):
        group = jnp.bitwise_xor(me, step)
        for h in range(LOCAL):
            out[0, :, head_columns(group, h)] = source[h]
    copies = pieces(out, out_hbm, sems)
    for copy in copies:
        copy.start()
    for copy in copies:
        copy.wait()


def unpack_pair_kernel(in0, in1, pair, turned, *rest):
    unpack_kernel(in0, in1, pair.at[0], turned.at[1], *rest)


def struct(*shape, dtype=bf16):
    return jax.ShapeDtypeStruct(shape, dtype)


HBM = pltpu.HBM
CUTS = 4


def call(kernel, name, outs, scratch=(), space=pltpu.VMEM, to=pltpu.VMEM):
    def run(*args):
        return pl.pallas_call(
            kernel,
            out_shape=jax.tree.map(lambda out: to(out.shape, out.dtype), outs),
            in_specs=[pl.BlockSpec(memory_space=space)] * len(args),
            out_specs=jax.tree.map(lambda _: pl.BlockSpec(memory_space=to), outs),
            scratch_shapes=scratch,
            compiler_params=pltpu.CompilerParams(vmem_limit_bytes=24 * 1024 * 1024),
            name=name,
        )(*(pltpu.with_memory_space_constraint(arg, space) for arg in args))

    return run


def after(array, *others):
    return lax.optimization_barrier((array, *others))[0]


def shards(query_rows, key_rows, value_rows, grad_output, block_lists):
    ctx = lax.axis_size("ctx")
    layers = ctx // TEAM
    width = query_rows.shape[2]

    def swap(array, step):
        return lax.ppermute(array, "ctx", [(i, i ^ step) for i in range(ctx)])

    def ring(array, flip):
        pairs = []
        for i in range(ctx):
            layer, up = i // TEAM, (i % 2) == flip
            inside = layer < layers - 1 if up else layer > 0
            pairs.append((i, (i + TEAM if up else i - TEAM) if inside else i ^ 1))
        return lax.ppermute(array, "ctx", pairs)

    part = struct(LOCAL, BLK, DH)
    qg = struct(LOCAL, QG, DH)
    team = struct(LOCAL, TEAM * BLK, DH)
    ends = struct(LOCAL, REACH * BLK, DH)
    slots = struct(LOCAL, SLOTS * BLK, DH)
    square = struct(LOCAL, SLOTS * BLK, TEAM * BLK)
    kept = struct(LOCAL, TEAM * BLK, DH, dtype=f32)
    rows_in = pltpu.VMEM((1, BLK, width), bf16)
    sems = pltpu.SemaphoreType.DMA((CUTS,))

    held = (rows_in, sems)
    k0, k1, k2, k3 = call(keys_kernel, "keys", (part,) * 4, held, HBM)(key_rows)
    value_rows = lax.optimization_barrier((value_rows, k0))[0]
    v0, qg0, one, v2, v3, qg2, qg3 = call(
        rest_kernel,
        "rest",
        (part, qg, struct(LOCAL, QG + BLK, DH), part, part, qg, qg),
        [pltpu.SMEM(block_lists.shape, jnp.int32), pltpu.SemaphoreType.DMA]
        + [rows_in] * 3
        + [pltpu.SemaphoreType.DMA((3, CUTS))],
        HBM,
    )(value_rows, query_rows, grad_output, block_lists)

    k2 = swap(k2, 2)
    k3 = swap(k3, 3)
    k1 = swap(k1, 1)
    qg23 = call(merge_kernel, "merge", struct(2, *qg.shape))(qg2, swap(qg3, 1))
    one = swap(one, 1)
    v2 = swap(after(v2, k2, k3), 2)
    v3 = swap(after(v3, k2, k3), 3)
    qg23 = swap(after(qg23, k2, k3), 2)

    def stage(base, *blocks):
        kernel = functools.partial(stage_kernel, base)
        local, first, second = call(kernel, "stage", (team, ends, ends))(*blocks)
        return local, ring(first, 0), ring(second, 1)

    k_local, k_halo1, k_halo2 = stage(0, k0, k1, k2, k3)
    v_local, v_halo1, v_halo2 = stage(QG, v0, one, v2, v3)
    probs, ks, qs, gs, dv_own, dv1, dv2 = call(
        probs_kernel,
        "probs",
        (square, slots, team, team, kept, ends, ends),
        [pltpu.VMEM((TEAM * MASK, DH), bf16), pltpu.VMEM((2 * REACH * BLK, DH), bf16)],
    )(qg0, one, qg23, k_local, k_halo1, k_halo2)

    def total(mine, first, second):
        return call(total_kernel, "total", (part,) * 4)(mine, ring(first, 0), ring(second, 1))

    def unpack(kernel, *parts):
        out = struct(1, BLK, width)
        return call(kernel, "unpack", out, held, to=HBM)(*parts)

    def home(parts):
        return unpack(unpack_kernel, parts[0], *(swap(parts[n], n) for n in range(1, TEAM)))

    grad_value = home(total(dv_own, dv1, dv2))
    sections = lax.axis_size("section")
    handoff = lax.ppermute(grad_value, "section", [(s + 1, s) for s in range(sections - 1)])

    dq0, dq1, dq23, dk_own, dk1, dk2 = call(
        grads_kernel,
        "grads",
        (part, part, struct(2, LOCAL, BLK, DH), kept, ends, ends),
        [
            pltpu.VMEM((LOCAL, SLOTS * BLK, DH), bf16),
            pltpu.VMEM((LOCAL, SLOTS * BLK, TEAM * BLK), bf16),
            pltpu.VMEM((TEAM * BLK, DH), bf16),
            pltpu.VMEM((2 * REACH * BLK, DH), bf16),
        ],
    )(probs, ks, qs, gs, v_local, v_halo1, v_halo2)
    dq23 = swap(dq23, 2)
    grad_query = unpack(unpack_pair_kernel, dq0, swap(dq1, 1), dq23, swap(dq23, 1))
    grad_key = home(total(dk_own, dk1, dk2))
    return (grad_query, grad_key, grad_value, handoff)


def solution(mesh):
    wide = P("section", "ctx", None)
    return jax.shard_map(
        shards,
        mesh=mesh,
        in_specs=(wide, wide, wide, wide, P("ctx", None)),
        out_specs=(wide,) * 4,
        check_vma=False,
    )
```

```python
import functools

import jax
import jax.numpy as jnp
from jax import lax
from jax.experimental import pallas as pl
from jax.experimental.pallas import tpu as pltpu
from jax.sharding import PartitionSpec as P

H = 12
DH = 128
BLK = 128
REACH = 2
TEAM = 4
LOCAL = H // TEAM
SPAN = 2 * REACH + 1
SLOTS = TEAM + 2 * REACH
SCALE = DH ** (-0.5)
LOG2E = 1.4426950408889634
OFF = -1e30
MASK = 16
K_AT, Q_AT, M_AT, G_AT, V_AT = 0, BLK, 2 * BLK, 2 * BLK + MASK, 3 * BLK + MASK
ALL = 4 * BLK + MASK
REST = ALL - BLK

bf16 = jnp.bfloat16
f32 = jnp.float32


def member():
    return lax.rem(lax.axis_index("ctx"), TEAM)


def rows_of(index, count=BLK):
    return pl.ds(pl.multiple_of(index * BLK, BLK), count)


def head_columns(group, h):
    return pl.ds(pl.multiple_of(group * (LOCAL * DH) + h * DH, DH), DH)


def pieces(source, target, sems):
    count = sems.shape[0]
    rows = BLK // count
    return [
        pltpu.make_async_copy(
            source.at[0, n * rows : (n + 1) * rows], target.at[0, n * rows : (n + 1) * rows], sems.at[n]
        )
        for n in range(count)
    ]


def cut(source, targets):
    me = member()
    for step, (target, base) in enumerate(targets):
        group = jnp.bitwise_xor(me, step)
        for h in range(LOCAL):
            target[h, base : base + BLK, :] = source[0, :, head_columns(group, h)]


def pack_kernel(
    k_hbm, q_hbm, g_hbm, v_hbm, lists_hbm, own, side, k2, k3, cross, lists, lists_sem, k, q, g, v, sems
):
    copies = [
        pieces(source, target, sems.at[n])
        for n, (source, target) in enumerate(((k_hbm, k), (q_hbm, q), (g_hbm, g), (v_hbm, v)))
    ]
    lists_copy = pltpu.make_async_copy(lists_hbm, lists, lists_sem)
    lists_copy.start()
    for group in copies:
        for copy in group:
            copy.start()
    block = lax.axis_index("ctx")
    lists_copy.wait()
    row = lax.broadcasted_iota(jnp.int32, (MASK, DH), 0)
    mask = jnp.full((MASK, DH), OFF, f32)
    for o in range(SPAN):
        wanted = jnp.int32(0)
        for n in range(lists.shape[1]):
            entry = lists[0, n]
            hit = (entry >= 0) & (entry == block + (o - REACH))
            wanted = jnp.maximum(wanted, hit.astype(jnp.int32))
        level = jnp.where(wanted > 0, 0.0, OFF).astype(f32)
        mask = jnp.where(row == o, level, mask)
    mask = mask.astype(bf16)
    for target, at in ((own, M_AT), (side, M_AT), (side, ALL + M_AT - BLK), (cross, M_AT - BLK)):
        for h in range(LOCAL):
            target[h, at : at + MASK, :] = mask
    targets = [((own, K_AT), (side, K_AT), (k2, 0), (k3, 0))]
    for at in (Q_AT, G_AT, V_AT):
        targets.append(((own, at), (side, at), (cross, at - BLK), (side, ALL + at - BLK)))
    for group, source, places in zip(copies, (k, q, g, v), targets):
        for copy in group:
            copy.wait()
        cut(source, places)


def merge_kernel(cross, side, q, g, v):
    for target, at, rows in ((q, Q_AT, BLK + MASK), (g, G_AT, BLK), (v, V_AT, BLK)):
        target[0] = cross[:, at - BLK : at - BLK + rows]
        target[1] = side[:, ALL + at - BLK : ALL + at - BLK + rows]


def stage_kernel(at, own, side, two, three, local, first, second):
    me = member()
    core = lax.rem(me, 2)
    for h in range(LOCAL):
        local[h, rows_of(me), :] = own[h, at : at + BLK]
        local[h, rows_of(jnp.bitwise_xor(me, 1)), :] = side[h, at : at + BLK]
        local[h, rows_of(jnp.bitwise_xor(me, 2)), :] = two[h]
        local[h, rows_of(jnp.bitwise_xor(me, 3)), :] = three[h]
    for h in range(LOCAL):
        first[h] = local[h, rows_of(REACH * (1 - core), REACH * BLK), :]
        second[h] = local[h, rows_of(REACH * core, REACH * BLK), :]


def stage_pair_kernel(at, own, side, pair, *outs):
    stage_kernel(at, own, side, pair.at[0], pair.at[1], *outs)


def nt(a, b):
    return lax.dot_general(a, b, (((1,), (1,)), ((), ())), preferred_element_type=f32)


def tn(a, b):
    return lax.dot_general(a, b, (((0,), (0,)), ((), ())), preferred_element_type=f32)


def nn(a, b):
    return lax.dot_general(a, b, (((1,), (0,)), ((), ())), preferred_element_type=f32)


def line_up(slots, h, local, first, second):
    core = lax.rem(member(), 2)
    top = REACH + TEAM
    slots[h, REACH * BLK : top * BLK, :] = local[h]
    slots[h, rows_of(core * top, REACH * BLK), :] = first[h]
    slots[h, rows_of((1 - core) * top, REACH * BLK), :] = second[h]


def key_sums(weights, rows, h, mine, ends, scale):
    for j in range(SLOTS):
        there = slice(j * BLK, (j + 1) * BLK)
        seen = slice(max(0, j - SPAN + 1) * BLK, (min(TEAM - 1, j) + 1) * BLK)
        term = nn(weights[h, there, seen], rows[h, seen, :])
        if scale is not None:
            term = term * scale
        if REACH <= j < REACH + TEAM:
            mine[h, (j - REACH) * BLK : (j - REACH + 1) * BLK, :] = term
        else:
            at = j if j < REACH else j - TEAM
            ends[at * BLK : (at + 1) * BLK, :] = term.astype(bf16)


def hand_ends(h, ends, first, second):
    core = lax.rem(member(), 2)
    first[h] = ends[rows_of(REACH * (1 - core), REACH * BLK), :]
    second[h] = ends[rows_of(REACH * core, REACH * BLK), :]


def probs_kernel(own, side, crossed, local, halo1, halo2, probs, ks, qs, bs):
    me = member()
    sources = ((own, Q_AT), (side, Q_AT), (crossed.at[0], 0), (crossed.at[1], 0))
    for h in range(LOCAL):
        line_up(ks, h, local, halo1, halo2)
        for step, (source, at) in enumerate(sources):
            position = jnp.bitwise_xor(me, step)
            qs[h, rows_of(position), :] = source[h, at : at + BLK]
            if h == 0:
                masks = pl.ds(pl.multiple_of(position * MASK, MASK), MASK)
                bs[masks, :] = source[h, at + BLK : at + BLK + MASK]
    for h in range(LOCAL):
        for pair in range(TEAM // 2):
            first = 2 * pair
            keys = ks[h, first * BLK : (first + SPAN + 1) * BLK, :]
            query = qs[h, first * BLK : (first + 2) * BLK, :]
            both = nt(keys, query)
            for n in range(2):
                i = first + n
                here = slice(i * BLK, (i + 1) * BLK)
                reach = slice(i * BLK, (i + SPAN) * BLK)
                bias = bs[i * MASK : (i + 1) * MASK, :].astype(f32)
                lanes = slice(n * BLK, (n + 1) * BLK)
                scores = jnp.concatenate(
                    [
                        both[(n + o) * BLK : (n + o + 1) * BLK, lanes] * (SCALE * LOG2E)
                        + bias[o : o + 1]
                        for o in range(SPAN)
                    ],
                    axis=0,
                )
                highest = jnp.max(scores, axis=0, keepdims=True)
                weights = jnp.exp2(scores - highest)
                scaled = weights * (1.0 / jnp.sum(weights, axis=0, keepdims=True))
                probs[h, reach, here] = scaled.astype(bf16)


def values_kernel(probs, own, side, crossed, gs, dv_own, dv1, dv2, ends):
    me = member()
    sources = ((own, G_AT), (side, G_AT), (crossed.at[0], 0), (crossed.at[1], 0))
    for h in range(LOCAL):
        for step, (source, at) in enumerate(sources):
            gs[h, rows_of(jnp.bitwise_xor(me, step)), :] = source[h, at : at + BLK]
        key_sums(probs, gs, h, dv_own, ends, None)
        hand_ends(h, ends, dv1, dv2)


def grads_kernel(
    probs, ks, qs, gs, local, halo1, halo2, dq0, dq1, dq23, dk_own, dk1, dk2, vs, ss, dqs, ends
):
    me = member()
    for h in range(LOCAL):
        line_up(vs, h, local, halo1, halo2)
        for pair in range(TEAM // 2):
            first = 2 * pair
            values = vs[h, first * BLK : (first + SPAN + 1) * BLK, :]
            grad = gs[h, first * BLK : (first + 2) * BLK, :]
            both = nt(values, grad)
            for n in range(2):
                i = first + n
                here = slice(i * BLK, (i + 1) * BLK)
                reach = slice(i * BLK, (i + SPAN) * BLK)
                grad_probs = both[n * BLK : (n + SPAN) * BLK, n * BLK : (n + 1) * BLK]
                weights = probs[h, reach, here].astype(f32)
                delta = jnp.sum(weights * grad_probs, axis=0, keepdims=True)
                scores_low = (weights * (grad_probs - delta)).astype(bf16)
                ss[h, reach, here] = scores_low
                dqs[here, :] = (tn(scores_low, ks[h, reach, :]) * SCALE).astype(bf16)
        for step, target in enumerate((dq0, dq1, dq23.at[0], dq23.at[1])):
            target[h] = dqs[rows_of(jnp.bitwise_xor(me, step)), :]
        key_sums(ss, qs, h, dk_own, ends, SCALE)
        hand_ends(h, ends, dk1, dk2)


def total_kernel(mine, ring1, ring2, *outs):
    me = member()
    core = lax.rem(me, 2)
    for step in range(TEAM):
        block = jnp.bitwise_xor(me, step)
        use1 = block // REACH == core
        at = rows_of(lax.rem(block, REACH))
        for h in range(LOCAL):
            term = jnp.where(use1, ring1[h, at, :].astype(f32), ring2[h, at, :].astype(f32))
            outs[step][h] = (mine[h, rows_of(block), :] + term).astype(bf16)


def total_pairs_kernel(mine, ring1, ring2, stay, give):
    total_kernel(mine, ring1, ring2, stay.at[0], give.at[0], stay.at[1], give.at[1])


def join_kernel(stay, got, out):
    out[0] = stay[1]
    out[1] = got[1]


def gather_kernel(in0, in1, in2, in3, groups):
    me = member()
    for step, source in enumerate((in0, in1, in2, in3)):
        groups[jnp.bitwise_xor(me, step)] = source[...]


def write_out(parts, out, out_hbm, sems):
    for group, source in parts:
        for h in range(LOCAL):
            out[0, :, head_columns(group, h)] = source[h]
    copies = pieces(out, out_hbm, sems)
    for copy in copies:
        copy.start()
    for copy in copies:
        copy.wait()


def unpack_kernel(in0, in1, in2, in3, out_hbm, out, sems):
    me = member()
    sources = (in0, in1, in2, in3)
    parts = [(jnp.bitwise_xor(me, step), source) for step, source in enumerate(sources)]
    write_out(parts, out, out_hbm, sems)


def unpack_joined_kernel(stay, got, crossed, *rest):
    unpack_kernel(stay.at[0], got.at[0], crossed.at[0], crossed.at[1], *rest)


def unpack_turned_kernel(dq0, dq1, crossed, turned, *rest):
    unpack_kernel(dq0, dq1, crossed.at[0], turned.at[1], *rest)


def unpack_groups_kernel(groups, out_hbm, out, sems):
    write_out([(group, groups.at[group]) for group in range(TEAM)], out, out_hbm, sems)


def struct(*shape, dtype=bf16):
    return jax.ShapeDtypeStruct(shape, dtype)


HBM = pltpu.HBM
CUTS = 4


def call(kernel, name, outs, scratch=(), space=pltpu.VMEM, to=pltpu.VMEM):
    def run(*args):
        return pl.pallas_call(
            kernel,
            out_shape=jax.tree.map(lambda out: to(out.shape, out.dtype), outs),
            in_specs=[pl.BlockSpec(memory_space=space)] * len(args),
            out_specs=jax.tree.map(lambda _: pl.BlockSpec(memory_space=to), outs),
            scratch_shapes=scratch,
            compiler_params=pltpu.CompilerParams(vmem_limit_bytes=24 * 1024 * 1024),
            name=name,
        )(*(pltpu.with_memory_space_constraint(arg, space) for arg in args))

    return run


def after(array, *others):
    return lax.optimization_barrier((array, *others))[0]


def shards(query_rows, key_rows, value_rows, grad_output, block_lists):
    ctx = lax.axis_size("ctx")
    layers = ctx // TEAM
    width = query_rows.shape[2]

    def swap(array, step):
        return lax.ppermute(array, "ctx", [(i, i ^ step) for i in range(ctx)])

    def ring(array, flip):
        pairs = []
        for i in range(ctx):
            layer, up = i // TEAM, (i % 2) == flip
            inside = layer < layers - 1 if up else layer > 0
            pairs.append((i, (i + TEAM if up else i - TEAM) if inside else i ^ 1))
        return lax.ppermute(array, "ctx", pairs)

    part = struct(LOCAL, BLK, DH)
    pair = struct(2, LOCAL, BLK, DH)
    team = struct(LOCAL, TEAM * BLK, DH)
    ends = struct(LOCAL, REACH * BLK, DH)
    slots = struct(LOCAL, SLOTS * BLK, DH)
    square = struct(LOCAL, SLOTS * BLK, TEAM * BLK)
    kept = struct(LOCAL, TEAM * BLK, DH, dtype=f32)
    rows_in = pltpu.VMEM((1, BLK, width), bf16)
    ends_in = pltpu.VMEM((2 * REACH * BLK, DH), bf16)

    own, side, k2, k3, cross = call(
        pack_kernel,
        "pack",
        (struct(LOCAL, ALL, DH), struct(LOCAL, ALL + REST, DH), part, part, struct(LOCAL, REST, DH)),
        [pltpu.SMEM(block_lists.shape, jnp.int32), pltpu.SemaphoreType.DMA]
        + [rows_in] * 4
        + [pltpu.SemaphoreType.DMA((4, CUTS))],
        HBM,
    )(key_rows, query_rows, grad_output, value_rows, block_lists)
    k2 = swap(k2, 2)
    k3 = swap(k3, 3)
    side = swap(side, 1)
    q23, g23, v23 = call(
        merge_kernel, "merge", (struct(2, LOCAL, BLK + MASK, DH), pair, pair)
    )(cross, side)

    def stage(kernel, *blocks):
        local, first, second = call(kernel, "stage", (team, ends, ends))(*blocks)
        return local, ring(first, 0), ring(second, 1)

    k_local, k_halo1, k_halo2 = stage(functools.partial(stage_kernel, K_AT), own, side, k2, k3)
    q23 = swap(after(q23, k_local), 2)
    g23 = swap(after(g23, k_local), 2)
    v23 = swap(v23, 2)
    v_local, v_halo1, v_halo2 = stage(functools.partial(stage_pair_kernel, V_AT), own, side, v23)
    probs, ks, qs = call(
        probs_kernel, "probs", (square, slots, team), [pltpu.VMEM((TEAM * MASK, DH), bf16)]
    )(own, side, q23, k_local, k_halo1, k_halo2)
    g23 = after(g23, v_halo1, v_halo2)
    gs, dv_own, dv1, dv2 = call(values_kernel, "values", (team, kept, ends, ends), [ends_in])(
        probs, own, side, g23
    )

    def total(kernel, outs, mine, first, second):
        return call(kernel, "total", outs)(mine, ring(first, 0), ring(second, 1))

    def unpack(kernel, *parts):
        out = struct(1, BLK, width)
        sems = pltpu.SemaphoreType.DMA((CUTS,))
        return call(kernel, "unpack", out, [rows_in, sems], to=HBM)(*parts)

    dq0, dq1, dq23, dk_own, dk1, dk2 = call(
        grads_kernel,
        "grads",
        (part, part, pair, kept, ends, ends),
        [
            pltpu.VMEM((LOCAL, SLOTS * BLK, DH), bf16),
            pltpu.VMEM((LOCAL, SLOTS * BLK, TEAM * BLK), bf16),
            pltpu.VMEM((TEAM * BLK, DH), bf16),
            ends_in,
        ],
    )(probs, ks, qs, gs, v_local, v_halo1, v_halo2)
    dv_own = after(dv_own, dk_own)
    dv = total(total_kernel, (part,) * 4, dv_own, dv1, dv2)
    dv_first = dv[0]
    dv = [dv[0]] + [swap(dv[step], step) for step in range(1, TEAM)]
    dv = call(gather_kernel, "gather", struct(TEAM, LOCAL, BLK, DH))(*dv)
    sections = lax.axis_size("section")
    passed = lax.ppermute(dv, "section", [(s + 1, s) for s in range(sections - 1)])
    grad_value = unpack(unpack_groups_kernel, dv)

    dq23 = swap(dq23, 2)
    dk_own = after(dk_own, dv_first)
    stay, give = total(total_pairs_kernel, (pair, pair), dk_own, dk1, dk2)
    got = swap(give, 1)
    joined = call(join_kernel, "join", pair)(after(stay, dv), got)
    crossed = swap(joined, 2)
    dq23 = after(dq23, got)
    grad_query = unpack(unpack_turned_kernel, dq0, swap(dq1, 1), dq23, swap(dq23, 1))
    stay = after(stay, grad_query, grad_value)
    grad_key = unpack(unpack_joined_kernel, stay, got, crossed)
    passed = after(passed, grad_key)
    handoff = unpack(unpack_groups_kernel, passed)
    return (grad_query, grad_key, grad_value, handoff)


def solution(mesh):
    wide = P("section", "ctx", None)
    return jax.shard_map(
        shards,
        mesh=mesh,
        in_specs=(wide, wide, wide, wide, P("ctx", None)),
        out_specs=(wide,) * 4,
        check_vma=False,
    )
```

```python
import functools

import jax
import jax.numpy as jnp
from jax import lax
from jax.experimental import pallas as pl
from jax.experimental.pallas import tpu as pltpu
from jax.sharding import PartitionSpec as P

H = 12
DH = 128
BLK = 128
REACH = 2
TEAM = 4
LOCAL = H // TEAM
SPAN = 2 * REACH + 1
SLOTS = TEAM + 2 * REACH
SCALE = DH ** (-0.5)
LOG2E = 1.4426950408889634
OFF = -1e30
MASK = 16
K_AT, Q_AT, M_AT, G_AT, V_AT = 0, BLK, 2 * BLK, 2 * BLK + MASK, 3 * BLK + MASK
ALL = 4 * BLK + MASK
REST = ALL - BLK

bf16 = jnp.bfloat16
f32 = jnp.float32


def member():
    return lax.rem(lax.axis_index("ctx"), TEAM)


def rows_of(index, count=BLK):
    return pl.ds(pl.multiple_of(index * BLK, BLK), count)


def head_columns(group, h):
    return pl.ds(pl.multiple_of(group * (LOCAL * DH) + h * DH, DH), DH)


def pieces(source, target, sems):
    count = sems.shape[0]
    rows = BLK // count
    return [
        pltpu.make_async_copy(
            source.at[0, n * rows : (n + 1) * rows], target.at[0, n * rows : (n + 1) * rows], sems.at[n]
        )
        for n in range(count)
    ]


def cut(source, targets):
    me = member()
    for step, (target, base) in enumerate(targets):
        group = jnp.bitwise_xor(me, step)
        for h in range(LOCAL):
            target[h, base : base + BLK, :] = source[0, :, head_columns(group, h)]


def pack_kernel(
    k_hbm, q_hbm, g_hbm, v_hbm, lists_hbm, own, side, k2, k3, cross, lists, lists_sem, k, q, g, v, sems
):
    copies = [
        pieces(source, target, sems.at[n])
        for n, (source, target) in enumerate(((k_hbm, k), (q_hbm, q), (g_hbm, g), (v_hbm, v)))
    ]
    lists_copy = pltpu.make_async_copy(lists_hbm, lists, lists_sem)
    lists_copy.start()
    for group in copies:
        for copy in group:
            copy.start()
    block = lax.axis_index("ctx")
    lists_copy.wait()
    row = lax.broadcasted_iota(jnp.int32, (MASK, DH), 0)
    mask = jnp.full((MASK, DH), OFF, f32)
    for o in range(SPAN):
        wanted = jnp.int32(0)
        for n in range(lists.shape[1]):
            entry = lists[0, n]
            hit = (entry >= 0) & (entry == block + (o - REACH))
            wanted = jnp.maximum(wanted, hit.astype(jnp.int32))
        level = jnp.where(wanted > 0, 0.0, OFF).astype(f32)
        mask = jnp.where(row == o, level, mask)
    mask = mask.astype(bf16)
    for target, at in ((own, M_AT), (side, M_AT), (side, ALL + M_AT - BLK), (cross, M_AT - BLK)):
        for h in range(LOCAL):
            target[h, at : at + MASK, :] = mask
    targets = [((own, K_AT), (side, K_AT), (k2, 0), (k3, 0))]
    for at in (Q_AT, G_AT, V_AT):
        targets.append(((own, at), (side, at), (cross, at - BLK), (side, ALL + at - BLK)))
    for group, source, places in zip(copies, (k, q, g, v), targets):
        for copy in group:
            copy.wait()
        cut(source, places)


def merge_kernel(cross, side, q, g, v):
    for target, at, rows in ((q, Q_AT, BLK + MASK), (g, G_AT, BLK), (v, V_AT, BLK)):
        target[0] = cross[:, at - BLK : at - BLK + rows]
        target[1] = side[:, ALL + at - BLK : ALL + at - BLK + rows]


def stage_kernel(at, own, side, two, three, local, first, second):
    me = member()
    core = lax.rem(me, 2)
    for h in range(LOCAL):
        local[h, rows_of(me), :] = own[h, at : at + BLK]
        local[h, rows_of(jnp.bitwise_xor(me, 1)), :] = side[h, at : at + BLK]
        local[h, rows_of(jnp.bitwise_xor(me, 2)), :] = two[h]
        local[h, rows_of(jnp.bitwise_xor(me, 3)), :] = three[h]
    for h in range(LOCAL):
        first[h] = local[h, rows_of(REACH * (1 - core), REACH * BLK), :]
        second[h] = local[h, rows_of(REACH * core, REACH * BLK), :]


def stage_pair_kernel(at, own, side, pair, *outs):
    stage_kernel(at, own, side, pair.at[0], pair.at[1], *outs)


def nt(a, b):
    return lax.dot_general(a, b, (((1,), (1,)), ((), ())), preferred_element_type=f32)


def tn(a, b):
    return lax.dot_general(a, b, (((0,), (0,)), ((), ())), preferred_element_type=f32)


def nn(a, b):
    return lax.dot_general(a, b, (((1,), (0,)), ((), ())), preferred_element_type=f32)


def line_up(slots, h, local, first, second):
    core = lax.rem(member(), 2)
    top = REACH + TEAM
    slots[h, REACH * BLK : top * BLK, :] = local[h]
    slots[h, rows_of(core * top, REACH * BLK), :] = first[h]
    slots[h, rows_of((1 - core) * top, REACH * BLK), :] = second[h]


def key_sums(weights, rows, h, mine, ends, scale):
    for j in range(SLOTS):
        there = slice(j * BLK, (j + 1) * BLK)
        seen = slice(max(0, j - SPAN + 1) * BLK, (min(TEAM - 1, j) + 1) * BLK)
        term = nn(weights[h, there, seen], rows[h, seen, :])
        if scale is not None:
            term = term * scale
        if REACH <= j < REACH + TEAM:
            mine[h, (j - REACH) * BLK : (j - REACH + 1) * BLK, :] = term
        else:
            at = j if j < REACH else j - TEAM
            ends[at * BLK : (at + 1) * BLK, :] = term.astype(bf16)


def hand_ends(h, ends, first, second):
    core = lax.rem(member(), 2)
    first[h] = ends[rows_of(REACH * (1 - core), REACH * BLK), :]
    second[h] = ends[rows_of(REACH * core, REACH * BLK), :]


def probs_kernel(own, side, crossed, local, halo1, halo2, probs, ks, qs, bs):
    me = member()
    sources = ((own, Q_AT), (side, Q_AT), (crossed.at[0], 0), (crossed.at[1], 0))
    for h in range(LOCAL):
        line_up(ks, h, local, halo1, halo2)
        for step, (source, at) in enumerate(sources):
            position = jnp.bitwise_xor(me, step)
            qs[h, rows_of(position), :] = source[h, at : at + BLK]
            if h == 0:
                masks = pl.ds(pl.multiple_of(position * MASK, MASK), MASK)
                bs[masks, :] = source[h, at + BLK : at + BLK + MASK]
    for h in range(LOCAL):
        for pair in range(TEAM // 2):
            first = 2 * pair
            keys = ks[h, first * BLK : (first + SPAN + 1) * BLK, :]
            query = qs[h, first * BLK : (first + 2) * BLK, :]
            both = nt(keys, query)
            for n in range(2):
                i = first + n
                here = slice(i * BLK, (i + 1) * BLK)
                reach = slice(i * BLK, (i + SPAN) * BLK)
                bias = bs[i * MASK : (i + 1) * MASK, :].astype(f32)
                lanes = slice(n * BLK, (n + 1) * BLK)
                scores = jnp.concatenate(
                    [
                        both[(n + o) * BLK : (n + o + 1) * BLK, lanes] * (SCALE * LOG2E)
                        + bias[o : o + 1]
                        for o in range(SPAN)
                    ],
                    axis=0,
                )
                highest = jnp.max(scores, axis=0, keepdims=True)
                weights = jnp.exp2(scores - highest)
                scaled = weights * (1.0 / jnp.sum(weights, axis=0, keepdims=True))
                probs[h, reach, here] = scaled.astype(bf16)


def values_kernel(probs, own, side, crossed, gs, dv_own, dv1, dv2, ends):
    me = member()
    sources = ((own, G_AT), (side, G_AT), (crossed.at[0], 0), (crossed.at[1], 0))
    for h in range(LOCAL):
        for step, (source, at) in enumerate(sources):
            gs[h, rows_of(jnp.bitwise_xor(me, step)), :] = source[h, at : at + BLK]
        key_sums(probs, gs, h, dv_own, ends, None)
        hand_ends(h, ends, dv1, dv2)


def scores_kernel(probs, qs, gs, local, halo1, halo2, ss, dk_own, dk1, dk2, vs, ends):
    for h in range(LOCAL):
        line_up(vs, h, local, halo1, halo2)
        for pair in range(TEAM // 2):
            first = 2 * pair
            values = vs[h, first * BLK : (first + SPAN + 1) * BLK, :]
            grad = gs[h, first * BLK : (first + 2) * BLK, :]
            both = nt(values, grad)
            for n in range(2):
                i = first + n
                here = slice(i * BLK, (i + 1) * BLK)
                reach = slice(i * BLK, (i + SPAN) * BLK)
                grad_probs = both[n * BLK : (n + SPAN) * BLK, n * BLK : (n + 1) * BLK]
                weights = probs[h, reach, here].astype(f32)
                delta = jnp.sum(weights * grad_probs, axis=0, keepdims=True)
                ss[h, reach, here] = (weights * (grad_probs - delta)).astype(bf16)
        key_sums(ss, qs, h, dk_own, ends, SCALE)
        hand_ends(h, ends, dk1, dk2)


def queries_kernel(ss, ks, dq0, dq1, dq23, dqs):
    me = member()
    for h in range(LOCAL):
        for i in range(TEAM):
            here = slice(i * BLK, (i + 1) * BLK)
            reach = slice(i * BLK, (i + SPAN) * BLK)
            dqs[here, :] = (tn(ss[h, reach, here], ks[h, reach, :]) * SCALE).astype(bf16)
        for step, target in enumerate((dq0, dq1, dq23.at[0], dq23.at[1])):
            target[h] = dqs[rows_of(jnp.bitwise_xor(me, step)), :]


def total_kernel(mine, ring1, ring2, *outs):
    me = member()
    core = lax.rem(me, 2)
    for step in range(TEAM):
        block = jnp.bitwise_xor(me, step)
        use1 = block // REACH == core
        at = rows_of(lax.rem(block, REACH))
        for h in range(LOCAL):
            term = jnp.where(use1, ring1[h, at, :].astype(f32), ring2[h, at, :].astype(f32))
            outs[step][h] = (mine[h, rows_of(block), :] + term).astype(bf16)


def total_pairs_kernel(mine, ring1, ring2, stay, give):
    total_kernel(mine, ring1, ring2, stay.at[0], give.at[0], stay.at[1], give.at[1])


def join_kernel(stay, got, out):
    out[0] = stay[1]
    out[1] = got[1]


def gather_kernel(in0, in1, in2, in3, groups):
    me = member()
    for step, source in enumerate((in0, in1, in2, in3)):
        groups[jnp.bitwise_xor(me, step)] = source[...]


def send_rows(out, out_hbm, sems):
    copies = pieces(out, out_hbm, sems)
    for copy in copies:
        copy.start()
    for copy in copies:
        copy.wait()


def write_out(parts, out, out_hbm, sems):
    for group, source in parts:
        for h in range(LOCAL):
            out[0, :, head_columns(group, h)] = source[h]
    send_rows(out, out_hbm, sems)


def unpack_kernel(in0, in1, in2, in3, out_hbm, out, sems):
    me = member()
    sources = (in0, in1, in2, in3)
    parts = [(jnp.bitwise_xor(me, step), source) for step, source in enumerate(sources)]
    write_out(parts, out, out_hbm, sems)


def unpack_joined_kernel(stay, got, crossed, *rest):
    unpack_kernel(stay.at[0], got.at[0], crossed.at[0], crossed.at[1], *rest)


def unpack_turned_kernel(dq0, dq1, crossed, turned, *rest):
    unpack_kernel(dq0, dq1, crossed.at[0], turned.at[1], *rest)


def unpack_passed_kernel(groups, out_hbm, out, sems):
    last = lax.axis_index("section") == lax.axis_size("section") - 1
    for group in range(TEAM):
        for h in range(LOCAL):
            source = groups[group, h]
            out[0, :, head_columns(group, h)] = jnp.where(last, jnp.zeros_like(source), source)
    send_rows(out, out_hbm, sems)


def struct(*shape, dtype=bf16):
    return jax.ShapeDtypeStruct(shape, dtype)


HBM = pltpu.HBM
CUTS = 4


def call(kernel, name, outs, scratch=(), space=pltpu.VMEM, to=pltpu.VMEM):
    def run(*args):
        return pl.pallas_call(
            kernel,
            out_shape=jax.tree.map(lambda out: to(out.shape, out.dtype), outs),
            in_specs=[pl.BlockSpec(memory_space=space)] * len(args),
            out_specs=jax.tree.map(lambda _: pl.BlockSpec(memory_space=to), outs),
            scratch_shapes=scratch,
            compiler_params=pltpu.CompilerParams(vmem_limit_bytes=24 * 1024 * 1024),
            name=name,
        )(*(pltpu.with_memory_space_constraint(arg, space) for arg in args))

    return run


def after(array, *others):
    return lax.optimization_barrier((array, *others))[0]


def shards(query_rows, key_rows, value_rows, grad_output, block_lists):
    ctx = lax.axis_size("ctx")
    layers = ctx // TEAM
    width = query_rows.shape[2]

    def swap(array, step):
        return lax.ppermute(array, "ctx", [(i, i ^ step) for i in range(ctx)])

    def ring(array, flip):
        pairs = []
        for i in range(ctx):
            layer, up = i // TEAM, (i % 2) == flip
            inside = layer < layers - 1 if up else layer > 0
            pairs.append((i, (i + TEAM if up else i - TEAM) if inside else i ^ 1))
        return lax.ppermute(array, "ctx", pairs)

    part = struct(LOCAL, BLK, DH)
    pair = struct(2, LOCAL, BLK, DH)
    team = struct(LOCAL, TEAM * BLK, DH)
    ends = struct(LOCAL, REACH * BLK, DH)
    slots = struct(LOCAL, SLOTS * BLK, DH)
    square = struct(LOCAL, SLOTS * BLK, TEAM * BLK)
    kept = struct(LOCAL, TEAM * BLK, DH, dtype=f32)
    rows_in = pltpu.VMEM((1, BLK, width), bf16)
    ends_in = pltpu.VMEM((2 * REACH * BLK, DH), bf16)

    own, side, k2, k3, cross = call(
        pack_kernel,
        "pack",
        (struct(LOCAL, ALL, DH), struct(LOCAL, ALL + REST, DH), part, part, struct(LOCAL, REST, DH)),
        [pltpu.SMEM(block_lists.shape, jnp.int32), pltpu.SemaphoreType.DMA]
        + [rows_in] * 4
        + [pltpu.SemaphoreType.DMA((4, CUTS))],
        HBM,
    )(key_rows, query_rows, grad_output, value_rows, block_lists)
    k2 = swap(k2, 2)
    k3 = swap(k3, 3)
    side = swap(side, 1)
    q23, g23, v23 = call(
        merge_kernel, "merge", (struct(2, LOCAL, BLK + MASK, DH), pair, pair)
    )(cross, side)

    def stage(kernel, *blocks):
        local, first, second = call(kernel, "stage", (team, ends, ends))(*blocks)
        return local, ring(first, 0), ring(second, 1)

    k_local, k_halo1, k_halo2 = stage(functools.partial(stage_kernel, K_AT), own, side, k2, k3)
    q23 = swap(q23, 2)
    g23 = swap(after(g23, k2, k3), 2)
    v23 = swap(v23, 2)
    v_local, v_halo1, v_halo2 = stage(functools.partial(stage_pair_kernel, V_AT), own, side, v23)
    probs, ks, qs = call(
        probs_kernel, "probs", (square, slots, team), [pltpu.VMEM((TEAM * MASK, DH), bf16)]
    )(own, side, q23, k_local, k_halo1, k_halo2)
    g23 = after(g23, v_halo1, v_halo2)
    g23 = after(g23, v_halo1, v_halo2)
    gs, dv_own, dv1, dv2 = call(values_kernel, "values", (team, kept, ends, ends), [ends_in])(
        probs, own, side, g23
    )

    def total(kernel, outs, mine, first, second):
        return call(kernel, "total", outs)(mine, ring(first, 0), ring(second, 1))

    def unpack(kernel, *parts):
        out = struct(1, BLK, width)
        sems = pltpu.SemaphoreType.DMA((CUTS,))
        return call(kernel, "unpack", out, [rows_in, sems], to=HBM)(*parts)

    ss, dk_own, dk1, dk2 = call(
        scores_kernel,
        "scores",
        (square, kept, ends, ends),
        [pltpu.VMEM((LOCAL, SLOTS * BLK, DH), bf16), ends_in],
    )(probs, qs, gs, v_local, v_halo1, v_halo2)
    dv_own = after(dv_own, dk_own)
    dv = total(total_kernel, (part,) * 4, dv_own, dv1, dv2)
    dv_first = dv[0]
    dv = [dv[0]] + [swap(dv[step], step) for step in range(1, TEAM)]
    late = call(gather_kernel, "gather", struct(TEAM, LOCAL, BLK, DH))(*dv)
    sections = lax.axis_size("section")
    passed = lax.ppermute(late, "section", [(s, (s - 1) % sections) for s in range(sections)])
    grad_value = unpack(unpack_kernel, *dv)
    dq0, dq1, dq23 = call(
        queries_kernel, "queries", (part, part, pair), [pltpu.VMEM((TEAM * BLK, DH), bf16)]
    )(ss, ks)
    dq23 = swap(dq23, 2)
    dk_own = after(dk_own, dv_first)
    stay, give = total(total_pairs_kernel, (pair, pair), dk_own, dk1, dk2)
    got = swap(give, 1)
    joined = call(join_kernel, "join", pair)(stay, got)
    crossed = swap(joined, 2)
    dq23 = after(dq23, got)
    grad_query = unpack(unpack_turned_kernel, dq0, swap(dq1, 1), dq23, swap(dq23, 1))
    handoff = passed
    stay = after(stay, grad_query)
    grad_key = unpack(unpack_joined_kernel, stay, got, crossed)
    passed = after(passed, grad_key)
    handoff = unpack(unpack_passed_kernel, passed)
    return (grad_query, grad_key, grad_value, handoff)


def solution(mesh):
    wide = P("section", "ctx", None)
    return jax.shard_map(
        shards,
        mesh=mesh,
        in_specs=(wide, wide, wide, wide, P("ctx", None)),
        out_specs=(wide,) * 4,
        check_vma=False,
    )
```

```python
import functools

import jax
import jax.numpy as jnp
from jax import lax
from jax.experimental import pallas as pl
from jax.experimental.pallas import tpu as pltpu
from jax.sharding import PartitionSpec as P

H = 12
DH = 128
BLK = 128
REACH = 2
TEAM = 4
LOCAL = H // TEAM
SPAN = 2 * REACH + 1
SLOTS = TEAM + 2 * REACH
SCALE = DH ** (-0.5)
LOG2E = 1.4426950408889634
OFF = -1e30
MASK = 16
K_AT, Q_AT, M_AT, G_AT, V_AT = 0, BLK, 2 * BLK, 2 * BLK + MASK, 3 * BLK + MASK
ALL = 4 * BLK + MASK
REST = ALL - BLK

bf16 = jnp.bfloat16
f32 = jnp.float32


def member():
    return lax.rem(lax.axis_index("ctx"), TEAM)


def rows_of(index, count=BLK):
    return pl.ds(pl.multiple_of(index * BLK, BLK), count)


def head_columns(group, h):
    return pl.ds(pl.multiple_of(group * (LOCAL * DH) + h * DH, DH), DH)


def pieces(source, target, sems):
    count = sems.shape[0]
    rows = BLK // count
    return [
        pltpu.make_async_copy(
            source.at[0, n * rows : (n + 1) * rows], target.at[0, n * rows : (n + 1) * rows], sems.at[n]
        )
        for n in range(count)
    ]


def cut(source, targets):
    me = member()
    for step, (target, base) in enumerate(targets):
        group = jnp.bitwise_xor(me, step)
        for h in range(LOCAL):
            target[h, base : base + BLK, :] = source[0, :, head_columns(group, h)]


def pack_kernel(
    k_hbm, q_hbm, g_hbm, v_hbm, lists_hbm, own, side, k2, k3, cross, lists, lists_sem, k, q, g, v, sems
):
    copies = [
        pieces(source, target, sems.at[n])
        for n, (source, target) in enumerate(((k_hbm, k), (q_hbm, q), (g_hbm, g), (v_hbm, v)))
    ]
    lists_copy = pltpu.make_async_copy(lists_hbm, lists, lists_sem)
    lists_copy.start()
    for group in copies:
        for copy in group:
            copy.start()
    block = lax.axis_index("ctx")
    lists_copy.wait()
    row = lax.broadcasted_iota(jnp.int32, (MASK, DH), 0)
    mask = jnp.full((MASK, DH), OFF, f32)
    for o in range(SPAN):
        wanted = jnp.int32(0)
        for n in range(lists.shape[1]):
            entry = lists[0, n]
            hit = (entry >= 0) & (entry == block + (o - REACH))
            wanted = jnp.maximum(wanted, hit.astype(jnp.int32))
        level = jnp.where(wanted > 0, 0.0, OFF).astype(f32)
        mask = jnp.where(row == o, level, mask)
    mask = mask.astype(bf16)
    for target, at in ((own, M_AT), (side, M_AT), (side, ALL + M_AT - BLK), (cross, M_AT - BLK)):
        for h in range(LOCAL):
            target[h, at : at + MASK, :] = mask
    targets = [((own, K_AT), (side, K_AT), (k2, 0), (k3, 0))]
    for at in (Q_AT, G_AT, V_AT):
        targets.append(((own, at), (side, at), (cross, at - BLK), (side, ALL + at - BLK)))
    for group, source, places in zip(copies, (k, q, g, v), targets):
        for copy in group:
            copy.wait()
        cut(source, places)


def merge_kernel(cross, side, q, g, v):
    for target, at, rows in ((q, Q_AT, BLK + MASK), (g, G_AT, BLK), (v, V_AT, BLK)):
        target[0] = cross[:, at - BLK : at - BLK + rows]
        target[1] = side[:, ALL + at - BLK : ALL + at - BLK + rows]


def stage_kernel(at, own, side, two, three, local, first, second):
    me = member()
    core = lax.rem(me, 2)
    for h in range(LOCAL):
        local[h, rows_of(me), :] = own[h, at : at + BLK]
        local[h, rows_of(jnp.bitwise_xor(me, 1)), :] = side[h, at : at + BLK]
        local[h, rows_of(jnp.bitwise_xor(me, 2)), :] = two[h]
        local[h, rows_of(jnp.bitwise_xor(me, 3)), :] = three[h]
    for h in range(LOCAL):
        first[h] = local[h, rows_of(REACH * (1 - core), REACH * BLK), :]
        second[h] = local[h, rows_of(REACH * core, REACH * BLK), :]


def stage_pair_kernel(at, own, side, pair, *outs):
    stage_kernel(at, own, side, pair.at[0], pair.at[1], *outs)


def nt(a, b):
    return lax.dot_general(a, b, (((1,), (1,)), ((), ())), preferred_element_type=f32)


def tn(a, b):
    return lax.dot_general(a, b, (((0,), (0,)), ((), ())), preferred_element_type=f32)


def nn(a, b):
    return lax.dot_general(a, b, (((1,), (0,)), ((), ())), preferred_element_type=f32)


def line_up(slots, h, local, first, second):
    core = lax.rem(member(), 2)
    top = REACH + TEAM
    slots[h, REACH * BLK : top * BLK, :] = local[h]
    slots[h, rows_of(core * top, REACH * BLK), :] = first[h]
    slots[h, rows_of((1 - core) * top, REACH * BLK), :] = second[h]


def key_sums(weights, rows, h, mine, ends, scale):
    for j in range(SLOTS):
        there = slice(j * BLK, (j + 1) * BLK)
        seen = slice(max(0, j - SPAN + 1) * BLK, (min(TEAM - 1, j) + 1) * BLK)
        term = nn(weights[h, there, seen], rows[h, seen, :])
        if scale is not None:
            term = term * scale
        if REACH <= j < REACH + TEAM:
            mine[h, (j - REACH) * BLK : (j - REACH + 1) * BLK, :] = term
        else:
            at = j if j < REACH else j - TEAM
            ends[at * BLK : (at + 1) * BLK, :] = term.astype(bf16)


def hand_ends(h, ends, first, second):
    core = lax.rem(member(), 2)
    first[h] = ends[rows_of(REACH * (1 - core), REACH * BLK), :]
    second[h] = ends[rows_of(REACH * core, REACH * BLK), :]


def probs_kernel(own, side, crossed, local, halo1, halo2, probs, ks, qs, bs):
    me = member()
    sources = ((own, Q_AT), (side, Q_AT), (crossed.at[0], 0), (crossed.at[1], 0))
    for h in range(LOCAL):
        line_up(ks, h, local, halo1, halo2)
        for step, (source, at) in enumerate(sources):
            position = jnp.bitwise_xor(me, step)
            qs[h, rows_of(position), :] = source[h, at : at + BLK]
            if h == 0:
                masks = pl.ds(pl.multiple_of(position * MASK, MASK), MASK)
                bs[masks, :] = source[h, at + BLK : at + BLK + MASK]
    for h in range(LOCAL):
        for pair in range(TEAM // 2):
            first = 2 * pair
            keys = ks[h, first * BLK : (first + SPAN + 1) * BLK, :]
            query = qs[h, first * BLK : (first + 2) * BLK, :]
            both = nt(keys, query)
            for n in range(2):
                i = first + n
                here = slice(i * BLK, (i + 1) * BLK)
                reach = slice(i * BLK, (i + SPAN) * BLK)
                bias = bs[i * MASK : (i + 1) * MASK, :].astype(f32)
                lanes = slice(n * BLK, (n + 1) * BLK)
                scores = jnp.concatenate(
                    [
                        both[(n + o) * BLK : (n + o + 1) * BLK, lanes] * (SCALE * LOG2E)
                        + bias[o : o + 1]
                        for o in range(SPAN)
                    ],
                    axis=0,
                )
                highest = jnp.max(scores, axis=0, keepdims=True)
                weights = jnp.exp2(scores - highest)
                scaled = weights * (1.0 / jnp.sum(weights, axis=0, keepdims=True))
                probs[h, reach, here] = scaled.astype(bf16)


def values_kernel(probs, own, side, crossed, gs, dv_own, dv1, dv2, ends):
    me = member()
    sources = ((own, G_AT), (side, G_AT), (crossed.at[0], 0), (crossed.at[1], 0))
    for h in range(LOCAL):
        for step, (source, at) in enumerate(sources):
            gs[h, rows_of(jnp.bitwise_xor(me, step)), :] = source[h, at : at + BLK]
        key_sums(probs, gs, h, dv_own, ends, None)
        hand_ends(h, ends, dv1, dv2)


def scores_kernel(probs, qs, gs, local, halo1, halo2, ss, dk_own, dk1, dk2, vs, ends):
    for h in range(LOCAL):
        line_up(vs, h, local, halo1, halo2)
        for pair in range(TEAM // 2):
            first = 2 * pair
            values = vs[h, first * BLK : (first + SPAN + 1) * BLK, :]
            grad = gs[h, first * BLK : (first + 2) * BLK, :]
            both = nt(values, grad)
            for n in range(2):
                i = first + n
                here = slice(i * BLK, (i + 1) * BLK)
                reach = slice(i * BLK, (i + SPAN) * BLK)
                grad_probs = both[n * BLK : (n + SPAN) * BLK, n * BLK : (n + 1) * BLK]
                weights = probs[h, reach, here].astype(f32)
                delta = jnp.sum(weights * grad_probs, axis=0, keepdims=True)
                ss[h, reach, here] = (weights * (grad_probs - delta)).astype(bf16)
        key_sums(ss, qs, h, dk_own, ends, SCALE)
        hand_ends(h, ends, dk1, dk2)


def queries_kernel(ss, ks, dq0, dq1, dq23, dqs):
    me = member()
    for h in range(LOCAL):
        for i in range(TEAM):
            here = slice(i * BLK, (i + 1) * BLK)
            reach = slice(i * BLK, (i + SPAN) * BLK)
            dqs[here, :] = (tn(ss[h, reach, here], ks[h, reach, :]) * SCALE).astype(bf16)
        for step, target in enumerate((dq0, dq1, dq23.at[0], dq23.at[1])):
            target[h] = dqs[rows_of(jnp.bitwise_xor(me, step)), :]


def total_kernel(mine, ring1, ring2, *outs):
    me = member()
    core = lax.rem(me, 2)
    for step in range(TEAM):
        block = jnp.bitwise_xor(me, step)
        use1 = block // REACH == core
        at = rows_of(lax.rem(block, REACH))
        for h in range(LOCAL):
            term = jnp.where(use1, ring1[h, at, :].astype(f32), ring2[h, at, :].astype(f32))
            outs[step][h] = (mine[h, rows_of(block), :] + term).astype(bf16)


def total_pairs_kernel(mine, ring1, ring2, stay, give):
    total_kernel(mine, ring1, ring2, stay.at[0], give.at[0], stay.at[1], give.at[1])


def join_kernel(stay, got, out):
    out[0] = stay[1]
    out[1] = got[1]


def gather_kernel(in0, in1, in2, in3, groups):
    me = member()
    for step, source in enumerate((in0, in1, in2, in3)):
        groups[jnp.bitwise_xor(me, step)] = source[...]


def send_rows(out, out_hbm, sems):
    copies = pieces(out, out_hbm, sems)
    for copy in copies:
        copy.start()
    for copy in copies:
        copy.wait()


def write_out(parts, out, out_hbm, sems):
    for group, source in parts:
        for h in range(LOCAL):
            out[0, :, head_columns(group, h)] = source[h]
    send_rows(out, out_hbm, sems)


def unpack_kernel(in0, in1, in2, in3, out_hbm, out, sems):
    me = member()
    sources = (in0, in1, in2, in3)
    parts = [(jnp.bitwise_xor(me, step), source) for step, source in enumerate(sources)]
    write_out(parts, out, out_hbm, sems)


def unpack_joined_kernel(stay, got, crossed, *rest):
    unpack_kernel(stay.at[0], got.at[0], crossed.at[0], crossed.at[1], *rest)


def unpack_turned_kernel(dq0, dq1, crossed, turned, *rest):
    unpack_kernel(dq0, dq1, crossed.at[0], turned.at[1], *rest)


def unpack_passed_kernel(groups, out_hbm, out, sems):
    last = lax.axis_index("section") == lax.axis_size("section") - 1
    for group in range(TEAM):
        for h in range(LOCAL):
            source = groups[group, h]
            out[0, :, head_columns(group, h)] = jnp.where(last, jnp.zeros_like(source), source)
    send_rows(out, out_hbm, sems)


def struct(*shape, dtype=bf16):
    return jax.ShapeDtypeStruct(shape, dtype)


HBM = pltpu.HBM
CUTS = 4


def call(kernel, name, outs, scratch=(), space=pltpu.VMEM, to=pltpu.VMEM):
    def run(*args):
        return pl.pallas_call(
            kernel,
            out_shape=jax.tree.map(lambda out: to(out.shape, out.dtype), outs),
            in_specs=[pl.BlockSpec(memory_space=space)] * len(args),
            out_specs=jax.tree.map(lambda _: pl.BlockSpec(memory_space=to), outs),
            scratch_shapes=scratch,
            compiler_params=pltpu.CompilerParams(vmem_limit_bytes=24 * 1024 * 1024),
            name=name,
        )(*(pltpu.with_memory_space_constraint(arg, space) for arg in args))

    return run


def after(array, *others):
    return lax.optimization_barrier((array, *others))[0]


def shards(query_rows, key_rows, value_rows, grad_output, block_lists):
    ctx = lax.axis_size("ctx")
    layers = ctx // TEAM
    width = query_rows.shape[2]

    def swap(array, step):
        return lax.ppermute(array, "ctx", [(i, i ^ step) for i in range(ctx)])

    def ring(array, flip):
        pairs = []
        for i in range(ctx):
            layer, up = i // TEAM, (i % 2) == flip
            inside = layer < layers - 1 if up else layer > 0
            pairs.append((i, (i + TEAM if up else i - TEAM) if inside else i ^ 1))
        return lax.ppermute(array, "ctx", pairs)

    part = struct(LOCAL, BLK, DH)
    pair = struct(2, LOCAL, BLK, DH)
    team = struct(LOCAL, TEAM * BLK, DH)
    ends = struct(LOCAL, REACH * BLK, DH)
    slots = struct(LOCAL, SLOTS * BLK, DH)
    square = struct(LOCAL, SLOTS * BLK, TEAM * BLK)
    kept = struct(LOCAL, TEAM * BLK, DH, dtype=f32)
    rows_in = pltpu.VMEM((1, BLK, width), bf16)
    ends_in = pltpu.VMEM((2 * REACH * BLK, DH), bf16)

    own, side, k2, k3, cross = call(
        pack_kernel,
        "pack",
        (struct(LOCAL, ALL, DH), struct(LOCAL, ALL + REST, DH), part, part, struct(LOCAL, REST, DH)),
        [pltpu.SMEM(block_lists.shape, jnp.int32), pltpu.SemaphoreType.DMA]
        + [rows_in] * 4
        + [pltpu.SemaphoreType.DMA((4, CUTS))],
        HBM,
    )(key_rows, query_rows, grad_output, value_rows, block_lists)
    k2 = swap(k2, 2)
    k3 = swap(k3, 3)
    side = swap(side, 1)
    q23, g23, v23 = call(
        merge_kernel, "merge", (struct(2, LOCAL, BLK + MASK, DH), pair, pair)
    )(cross, side)

    def stage(kernel, *blocks):
        local, first, second = call(kernel, "stage", (team, ends, ends))(*blocks)
        return local, ring(first, 0), ring(second, 1)

    k_local, k_halo1, k_halo2 = stage(functools.partial(stage_kernel, K_AT), own, side, k2, k3)
    q23 = swap(q23, 2)
    g23 = swap(after(g23, k2, k3), 2)
    v23 = swap(v23, 2)
    v_local, v_halo1, v_halo2 = stage(functools.partial(stage_pair_kernel, V_AT), own, side, v23)
    probs, ks, qs = call(
        probs_kernel, "probs", (square, slots, team), [pltpu.VMEM((TEAM * MASK, DH), bf16)]
    )(own, side, q23, k_local, k_halo1, k_halo2)
    g23 = after(g23, v_halo1, v_halo2)
    gs, dv_own, dv1, dv2 = call(values_kernel, "values", (team, kept, ends, ends), [ends_in])(
        probs, own, side, g23
    )

    def total(kernel, outs, mine, first, second):
        return call(kernel, "total", outs)(mine, ring(first, 0), ring(second, 1))

    def unpack(kernel, *parts):
        out = struct(1, BLK, width)
        sems = pltpu.SemaphoreType.DMA((CUTS,))
        return call(kernel, "unpack", out, [rows_in, sems], to=HBM)(*parts)

    ss, dk_own, dk1, dk2 = call(
        scores_kernel,
        "scores",
        (square, kept, ends, ends),
        [pltpu.VMEM((LOCAL, SLOTS * BLK, DH), bf16), ends_in],
    )(probs, qs, gs, v_local, v_halo1, v_halo2)
    dv_own = after(dv_own, dk_own)
    dv = total(total_kernel, (part,) * 4, dv_own, dv1, dv2)
    dv_first = dv[0]
    dv = [dv[0]] + [swap(dv[step], step) for step in range(1, TEAM)]
    late = call(gather_kernel, "gather", struct(TEAM, LOCAL, BLK, DH))(*dv)
    sections = lax.axis_size("section")
    passed = lax.ppermute(late, "section", [(s, (s - 1) % sections) for s in range(sections)])
    dq0, dq1, dq23 = call(
        queries_kernel, "queries", (part, part, pair), [pltpu.VMEM((TEAM * BLK, DH), bf16)]
    )(after(ss, dv_first), ks)
    dq23 = swap(dq23, 2)
    stay, give = total(total_pairs_kernel, (pair, pair), dk_own, dk1, dk2)
    got = swap(give, 1)
    joined = call(join_kernel, "join", pair)(after(stay, late), got)
    crossed = swap(joined, 2)
    dv[0] = after(dv[0], joined)
    grad_value = unpack(unpack_kernel, *dv)
    dq23 = after(dq23, got)
    grad_query = unpack(unpack_turned_kernel, dq0, swap(dq1, 1), dq23, swap(dq23, 1))
    handoff = passed
    grad_key = unpack(unpack_joined_kernel, stay, got, crossed)
    passed = after(passed, grad_key)
    handoff = unpack(unpack_passed_kernel, passed)
    return (grad_query, grad_key, grad_value, handoff)


def solution(mesh):
    wide = P("section", "ctx", None)
    return jax.shard_map(
        shards,
        mesh=mesh,
        in_specs=(wide, wide, wide, wide, P("ctx", None)),
        out_specs=(wide,) * 4,
        check_vma=False,
    )
```

```python
import functools

import jax
import jax.numpy as jnp
from jax import lax
from jax.experimental import pallas as pl
from jax.experimental.pallas import tpu as pltpu
from jax.sharding import PartitionSpec as P

H = 12
DH = 128
BLK = 128
REACH = 2
TEAM = 4
LOCAL = H // TEAM
SPAN = 2 * REACH + 1
SLOTS = TEAM + 2 * REACH
SCALE = DH ** (-0.5)
LOG2E = 1.4426950408889634
OFF = -1e30
MASK = 16
K_AT, Q_AT, M_AT, G_AT, V_AT = 0, BLK, 2 * BLK, 2 * BLK + MASK, 3 * BLK + MASK
ALL = 4 * BLK + MASK
REST = ALL - BLK

bf16 = jnp.bfloat16
f32 = jnp.float32


def member():
    return lax.rem(lax.axis_index("ctx"), TEAM)


def rows_of(index, count=BLK):
    return pl.ds(pl.multiple_of(index * BLK, BLK), count)


def head_columns(group, h):
    return pl.ds(pl.multiple_of(group * (LOCAL * DH) + h * DH, DH), DH)


def pieces(source, target, sems):
    count = sems.shape[0]
    rows = BLK // count
    return [
        pltpu.make_async_copy(
            source.at[0, n * rows : (n + 1) * rows], target.at[0, n * rows : (n + 1) * rows], sems.at[n]
        )
        for n in range(count)
    ]


def cut(source, targets):
    me = member()
    for step, (target, base) in enumerate(targets):
        group = jnp.bitwise_xor(me, step)
        for h in range(LOCAL):
            target[h, base : base + BLK, :] = source[0, :, head_columns(group, h)]


def pack_kernel(
    k_hbm, q_hbm, g_hbm, v_hbm, lists_hbm, own, side, k2, k3, cross, lists, lists_sem, k, q, g, v, sems
):
    copies = [
        pieces(source, target, sems.at[n])
        for n, (source, target) in enumerate(((k_hbm, k), (q_hbm, q), (g_hbm, g), (v_hbm, v)))
    ]
    lists_copy = pltpu.make_async_copy(lists_hbm, lists, lists_sem)
    lists_copy.start()
    for group in copies:
        for copy in group:
            copy.start()
    block = lax.axis_index("ctx")
    lists_copy.wait()
    row = lax.broadcasted_iota(jnp.int32, (MASK, DH), 0)
    mask = jnp.full((MASK, DH), OFF, f32)
    for o in range(SPAN):
        wanted = jnp.int32(0)
        for n in range(lists.shape[1]):
            entry = lists[0, n]
            hit = (entry >= 0) & (entry == block + (o - REACH))
            wanted = jnp.maximum(wanted, hit.astype(jnp.int32))
        level = jnp.where(wanted > 0, 0.0, OFF).astype(f32)
        mask = jnp.where(row == o, level, mask)
    mask = mask.astype(bf16)
    for target, at in ((own, M_AT), (side, M_AT), (side, ALL + M_AT - BLK), (cross, M_AT - BLK)):
        for h in range(LOCAL):
            target[h, at : at + MASK, :] = mask
    targets = [((own, K_AT), (side, K_AT), (k2, 0), (k3, 0))]
    for at in (Q_AT, G_AT, V_AT):
        targets.append(((own, at), (side, at), (cross, at - BLK), (side, ALL + at - BLK)))
    for group, source, places in zip(copies, (k, q, g, v), targets):
        for copy in group:
            copy.wait()
        cut(source, places)


def merge_kernel(cross, side, q, g, v):
    for target, at, rows in ((q, Q_AT, BLK + MASK), (g, G_AT, BLK), (v, V_AT, BLK)):
        target[0] = cross[:, at - BLK : at - BLK + rows]
        target[1] = side[:, ALL + at - BLK : ALL + at - BLK + rows]


def stage_kernel(at, own, side, two, three, local, first, second):
    me = member()
    core = lax.rem(me, 2)
    for h in range(LOCAL):
        local[h, rows_of(me), :] = own[h, at : at + BLK]
        local[h, rows_of(jnp.bitwise_xor(me, 1)), :] = side[h, at : at + BLK]
        local[h, rows_of(jnp.bitwise_xor(me, 2)), :] = two[h]
        local[h, rows_of(jnp.bitwise_xor(me, 3)), :] = three[h]
    for h in range(LOCAL):
        first[h] = local[h, rows_of(REACH * (1 - core), REACH * BLK), :]
        second[h] = local[h, rows_of(REACH * core, REACH * BLK), :]


def stage_pair_kernel(at, own, side, pair, *outs):
    stage_kernel(at, own, side, pair.at[0], pair.at[1], *outs)


def nt(a, b):
    return lax.dot_general(a, b, (((1,), (1,)), ((), ())), preferred_element_type=f32)


def tn(a, b):
    return lax.dot_general(a, b, (((0,), (0,)), ((), ())), preferred_element_type=f32)


def nn(a, b):
    return lax.dot_general(a, b, (((1,), (0,)), ((), ())), preferred_element_type=f32)


def line_up(slots, h, local, first, second):
    core = lax.rem(member(), 2)
    top = REACH + TEAM
    slots[h, REACH * BLK : top * BLK, :] = local[h]
    slots[h, rows_of(core * top, REACH * BLK), :] = first[h]
    slots[h, rows_of((1 - core) * top, REACH * BLK), :] = second[h]


def key_sums(weights, rows, h, mine, ends, scale):
    for j in range(SLOTS):
        there = slice(j * BLK, (j + 1) * BLK)
        seen = slice(max(0, j - SPAN + 1) * BLK, (min(TEAM - 1, j) + 1) * BLK)
        term = nn(weights[h, there, seen], rows[h, seen, :])
        if scale is not None:
            term = term * scale
        if REACH <= j < REACH + TEAM:
            mine[h, (j - REACH) * BLK : (j - REACH + 1) * BLK, :] = term
        else:
            at = j if j < REACH else j - TEAM
            ends[at * BLK : (at + 1) * BLK, :] = term.astype(bf16)


def hand_ends(h, ends, first, second):
    core = lax.rem(member(), 2)
    first[h] = ends[rows_of(REACH * (1 - core), REACH * BLK), :]
    second[h] = ends[rows_of(REACH * core, REACH * BLK), :]


def probs_kernel(own, side, crossed, local, halo1, halo2, probs, ks, qs, bs):
    me = member()
    sources = ((own, Q_AT), (side, Q_AT), (crossed.at[0], 0), (crossed.at[1], 0))
    for h in range(LOCAL):
        line_up(ks, h, local, halo1, halo2)
        for step, (source, at) in enumerate(sources):
            position = jnp.bitwise_xor(me, step)
            qs[h, rows_of(position), :] = source[h, at : at + BLK]
            if h == 0:
                masks = pl.ds(pl.multiple_of(position * MASK, MASK), MASK)
                bs[masks, :] = source[h, at + BLK : at + BLK + MASK]
    for h in range(LOCAL):
        for pair in range(TEAM // 2):
            first = 2 * pair
            keys = ks[h, first * BLK : (first + SPAN + 1) * BLK, :]
            query = qs[h, first * BLK : (first + 2) * BLK, :]
            both = nt(keys, query)
            for n in range(2):
                i = first + n
                here = slice(i * BLK, (i + 1) * BLK)
                reach = slice(i * BLK, (i + SPAN) * BLK)
                bias = bs[i * MASK : (i + 1) * MASK, :].astype(f32)
                lanes = slice(n * BLK, (n + 1) * BLK)
                scores = jnp.concatenate(
                    [
                        both[(n + o) * BLK : (n + o + 1) * BLK, lanes] * (SCALE * LOG2E)
                        + bias[o : o + 1]
                        for o in range(SPAN)
                    ],
                    axis=0,
                )
                highest = jnp.max(scores, axis=0, keepdims=True)
                weights = jnp.exp2(scores - highest)
                scaled = weights * (1.0 / jnp.sum(weights, axis=0, keepdims=True))
                probs[h, reach, here] = scaled.astype(bf16)


def values_kernel(probs, own, side, crossed, gs, dv_own, dv1, dv2, ends):
    me = member()
    sources = ((own, G_AT), (side, G_AT), (crossed.at[0], 0), (crossed.at[1], 0))
    for h in range(LOCAL):
        for step, (source, at) in enumerate(sources):
            gs[h, rows_of(jnp.bitwise_xor(me, step)), :] = source[h, at : at + BLK]
        key_sums(probs, gs, h, dv_own, ends, None)
        hand_ends(h, ends, dv1, dv2)


def scores_kernel(probs, qs, gs, local, halo1, halo2, ss, dk_own, dk1, dk2, vs, ends):
    for h in range(LOCAL):
        line_up(vs, h, local, halo1, halo2)
        for pair in range(TEAM // 2):
            first = 2 * pair
            values = vs[h, first * BLK : (first + SPAN + 1) * BLK, :]
            grad = gs[h, first * BLK : (first + 2) * BLK, :]
            both = nt(values, grad)
            for n in range(2):
                i = first + n
                here = slice(i * BLK, (i + 1) * BLK)
                reach = slice(i * BLK, (i + SPAN) * BLK)
                grad_probs = both[n * BLK : (n + SPAN) * BLK, n * BLK : (n + 1) * BLK]
                weights = probs[h, reach, here].astype(f32)
                delta = jnp.sum(weights * grad_probs, axis=0, keepdims=True)
                ss[h, reach, here] = (weights * (grad_probs - delta)).astype(bf16)
        key_sums(ss, qs, h, dk_own, ends, SCALE)
        hand_ends(h, ends, dk1, dk2)


def queries_kernel(ss, ks, dq0, dq1, dq23, dqs):
    me = member()
    for h in range(LOCAL):
        for i in range(TEAM):
            here = slice(i * BLK, (i + 1) * BLK)
            reach = slice(i * BLK, (i + SPAN) * BLK)
            dqs[here, :] = (tn(ss[h, reach, here], ks[h, reach, :]) * SCALE).astype(bf16)
        for step, target in enumerate((dq0, dq1, dq23.at[0], dq23.at[1])):
            target[h] = dqs[rows_of(jnp.bitwise_xor(me, step)), :]


def total_kernel(mine, ring1, ring2, *outs):
    me = member()
    core = lax.rem(me, 2)
    for step in range(TEAM):
        block = jnp.bitwise_xor(me, step)
        use1 = block // REACH == core
        at = rows_of(lax.rem(block, REACH))
        for h in range(LOCAL):
            term = jnp.where(use1, ring1[h, at, :].astype(f32), ring2[h, at, :].astype(f32))
            outs[step][h] = (mine[h, rows_of(block), :] + term).astype(bf16)


def total_pairs_kernel(mine, ring1, ring2, stay, give):
    total_kernel(mine, ring1, ring2, stay.at[0], give.at[0], stay.at[1], give.at[1])


def join_kernel(stay, got, out):
    out[0] = stay[1]
    out[1] = got[1]


def gather_kernel(in0, in1, in2, in3, groups):
    me = member()
    for step, source in enumerate((in0, in1, in2, in3)):
        groups[jnp.bitwise_xor(me, step)] = source[...]


def write_out(parts, out, out_hbm, sems, wanted=None):
    copies = pieces(out, out_hbm, sems)
    count = BLK // len(copies)
    for n, copy in enumerate(copies):
        rows = slice(n * count, (n + 1) * count)
        for group, source in parts:
            for h in range(LOCAL):
                value = source[h, rows]
                if wanted is not None:
                    value = jnp.where(wanted, value, jnp.zeros_like(value))
                out[0, rows, head_columns(group, h)] = value
        copy.start()
    for copy in copies:
        copy.wait()


def unpack_kernel(in0, in1, in2, in3, out_hbm, out, sems):
    me = member()
    sources = (in0, in1, in2, in3)
    parts = [(jnp.bitwise_xor(me, step), source) for step, source in enumerate(sources)]
    write_out(parts, out, out_hbm, sems)


def unpack_joined_kernel(stay, got, crossed, *rest):
    unpack_kernel(stay.at[0], got.at[0], crossed.at[0], crossed.at[1], *rest)


def unpack_turned_kernel(dq0, dq1, crossed, turned, *rest):
    unpack_kernel(dq0, dq1, crossed.at[0], turned.at[1], *rest)


def unpack_passed_kernel(groups, out_hbm, out, sems):
    wanted = lax.axis_index("section") < lax.axis_size("section") - 1
    parts = [(group, groups.at[group]) for group in range(TEAM)]
    write_out(parts, out, out_hbm, sems, wanted)


def struct(*shape, dtype=bf16):
    return jax.ShapeDtypeStruct(shape, dtype)


HBM = pltpu.HBM
CUTS = 4


def call(kernel, name, outs, scratch=(), space=pltpu.VMEM, to=pltpu.VMEM):
    def run(*args):
        return pl.pallas_call(
            kernel,
            out_shape=jax.tree.map(lambda out: to(out.shape, out.dtype), outs),
            in_specs=[pl.BlockSpec(memory_space=space)] * len(args),
            out_specs=jax.tree.map(lambda _: pl.BlockSpec(memory_space=to), outs),
            scratch_shapes=scratch,
            compiler_params=pltpu.CompilerParams(vmem_limit_bytes=24 * 1024 * 1024),
            name=name,
        )(*(pltpu.with_memory_space_constraint(arg, space) for arg in args))

    return run


def after(array, *others):
    return lax.optimization_barrier((array, *others))[0]


def shards(query_rows, key_rows, value_rows, grad_output, block_lists):
    ctx = lax.axis_size("ctx")
    layers = ctx // TEAM
    width = query_rows.shape[2]

    def swap(array, step):
        return lax.ppermute(array, "ctx", [(i, i ^ step) for i in range(ctx)])

    def ring(array, flip):
        pairs = []
        for i in range(ctx):
            layer, up = i // TEAM, (i % 2) == flip
            inside = layer < layers - 1 if up else layer > 0
            pairs.append((i, (i + TEAM if up else i - TEAM) if inside else i ^ 1))
        return lax.ppermute(array, "ctx", pairs)

    part = struct(LOCAL, BLK, DH)
    pair = struct(2, LOCAL, BLK, DH)
    team = struct(LOCAL, TEAM * BLK, DH)
    ends = struct(LOCAL, REACH * BLK, DH)
    slots = struct(LOCAL, SLOTS * BLK, DH)
    square = struct(LOCAL, SLOTS * BLK, TEAM * BLK)
    kept = struct(LOCAL, TEAM * BLK, DH, dtype=f32)
    rows_in = pltpu.VMEM((1, BLK, width), bf16)
    ends_in = pltpu.VMEM((2 * REACH * BLK, DH), bf16)

    own, side, k2, k3, cross = call(
        pack_kernel,
        "pack",
        (struct(LOCAL, ALL, DH), struct(LOCAL, ALL + REST, DH), part, part, struct(LOCAL, REST, DH)),
        [pltpu.SMEM(block_lists.shape, jnp.int32), pltpu.SemaphoreType.DMA]
        + [rows_in] * 4
        + [pltpu.SemaphoreType.DMA((4, CUTS))],
        HBM,
    )(key_rows, query_rows, grad_output, value_rows, block_lists)
    k2 = swap(k2, 2)
    k3 = swap(k3, 3)
    side = swap(side, 1)
    q23, g23, v23 = call(
        merge_kernel, "merge", (struct(2, LOCAL, BLK + MASK, DH), pair, pair)
    )(cross, side)

    def stage(kernel, *blocks):
        local, first, second = call(kernel, "stage", (team, ends, ends))(*blocks)
        return local, ring(first, 0), ring(second, 1)

    k_local, k_halo1, k_halo2 = stage(functools.partial(stage_kernel, K_AT), own, side, k2, k3)
    q23 = swap(q23, 2)
    g23 = swap(after(g23, k2, k3), 2)
    v23 = swap(v23, 2)
    v_local, v_halo1, v_halo2 = stage(functools.partial(stage_pair_kernel, V_AT), own, side, v23)
    probs, ks, qs = call(
        probs_kernel, "probs", (square, slots, team), [pltpu.VMEM((TEAM * MASK, DH), bf16)]
    )(own, side, q23, k_local, k_halo1, k_halo2)
    g23 = after(g23, v_halo1, v_halo2)
    gs, dv_own, dv1, dv2 = call(values_kernel, "values", (team, kept, ends, ends), [ends_in])(
        probs, own, side, g23
    )

    def total(kernel, outs, mine, first, second):
        return call(kernel, "total", outs)(mine, ring(first, 0), ring(second, 1))

    def unpack(kernel, *parts):
        out = struct(1, BLK, width)
        sems = pltpu.SemaphoreType.DMA((CUTS,))
        return call(kernel, "unpack", out, [rows_in, sems], to=HBM)(*parts)

    ss, dk_own, dk1, dk2 = call(
        scores_kernel,
        "scores",
        (square, kept, ends, ends),
        [pltpu.VMEM((LOCAL, SLOTS * BLK, DH), bf16), ends_in],
    )(probs, qs, gs, v_local, v_halo1, v_halo2)
    dv_own = after(dv_own, dk_own)
    dv = total(total_kernel, (part,) * 4, dv_own, dv1, dv2)
    dv_first = dv[0]
    dv = [dv[0]] + [swap(dv[step], step) for step in range(1, TEAM)]
    late = call(gather_kernel, "gather", struct(TEAM, LOCAL, BLK, DH))(*dv)
    sections = lax.axis_size("section")
    passed = lax.ppermute(late, "section", [(s, (s - 1) % sections) for s in range(sections)])
    dq0, dq1, dq23 = call(
        queries_kernel, "queries", (part, part, pair), [pltpu.VMEM((TEAM * BLK, DH), bf16)]
    )(ss, ks)
    dq23 = after(dq23, dv_first)
    dq23 = swap(dq23, 2)
    stay, give = total(total_pairs_kernel, (pair, pair), dk_own, dk1, dk2)
    got = swap(give, 1)
    joined = call(join_kernel, "join", pair)(after(stay, late), got)
    crossed = swap(joined, 2)
    dv[0] = after(dv[0], joined)
    grad_value = unpack(unpack_kernel, *dv)
    dq23 = after(dq23, got)
    grad_query = unpack(unpack_turned_kernel, dq0, swap(dq1, 1), dq23, swap(dq23, 1))
    grad_key = unpack(unpack_joined_kernel, stay, got, crossed)
    handoff = unpack(unpack_passed_kernel, passed)
    return (grad_query, grad_key, grad_value, handoff)


def solution(mesh):
    wide = P("section", "ctx", None)
    return jax.shard_map(
        shards,
        mesh=mesh,
        in_specs=(wide, wide, wide, wide, P("ctx", None)),
        out_specs=(wide,) * 4,
        check_vma=False,
    )
```

```python
import functools

import jax
import jax.numpy as jnp
from jax import lax
from jax.experimental import pallas as pl
from jax.experimental.pallas import tpu as pltpu
from jax.sharding import PartitionSpec as P

H = 12
DH = 128
BLK = 128
REACH = 2
TEAM = 4
LOCAL = H // TEAM
SPAN = 2 * REACH + 1
SLOTS = TEAM + 2 * REACH
SCALE = DH ** (-0.5)
LOG2E = 1.4426950408889634
OFF = -1e30
MASK = 16
K_AT, Q_AT, M_AT, G_AT, V_AT = 0, BLK, 2 * BLK, 2 * BLK + MASK, 3 * BLK + MASK
ALL = 4 * BLK + MASK
REST = ALL - BLK

bf16 = jnp.bfloat16
f32 = jnp.float32


def member():
    return lax.rem(lax.axis_index("ctx"), TEAM)


def rows_of(index, count=BLK):
    return pl.ds(pl.multiple_of(index * BLK, BLK), count)


def head_columns(group, h):
    return pl.ds(pl.multiple_of(group * (LOCAL * DH) + h * DH, DH), DH)


def pieces(source, target, sems):
    count = sems.shape[0]
    rows = BLK // count
    return [
        pltpu.make_async_copy(
            source.at[0, n * rows : (n + 1) * rows], target.at[0, n * rows : (n + 1) * rows], sems.at[n]
        )
        for n in range(count)
    ]


def cut(source, targets):
    me = member()
    for step, (target, base) in enumerate(targets):
        group = jnp.bitwise_xor(me, step)
        for h in range(LOCAL):
            target[h, base : base + BLK, :] = source[0, :, head_columns(group, h)]


def pack_kernel(
    k_hbm, q_hbm, g_hbm, v_hbm, lists_hbm, own, side, k2, k3, cross, lists, lists_sem, k, q, g, v, sems
):
    copies = [
        pieces(source, target, sems.at[n])
        for n, (source, target) in enumerate(((k_hbm, k), (q_hbm, q), (g_hbm, g), (v_hbm, v)))
    ]
    lists_copy = pltpu.make_async_copy(lists_hbm, lists, lists_sem)
    lists_copy.start()
    for group in copies:
        for copy in group:
            copy.start()
    block = lax.axis_index("ctx")
    lists_copy.wait()
    row = lax.broadcasted_iota(jnp.int32, (MASK, DH), 0)
    mask = jnp.full((MASK, DH), OFF, f32)
    for o in range(SPAN):
        wanted = jnp.int32(0)
        for n in range(lists.shape[1]):
            entry = lists[0, n]
            hit = (entry >= 0) & (entry == block + (o - REACH))
            wanted = jnp.maximum(wanted, hit.astype(jnp.int32))
        level = jnp.where(wanted > 0, 0.0, OFF).astype(f32)
        mask = jnp.where(row == o, level, mask)
    mask = mask.astype(bf16)
    for target, at in ((own, M_AT), (side, M_AT), (side, ALL + M_AT - BLK), (cross, M_AT - BLK)):
        for h in range(LOCAL):
            target[h, at : at + MASK, :] = mask
    targets = [((own, K_AT), (side, K_AT), (k2, 0), (k3, 0))]
    for at in (Q_AT, G_AT, V_AT):
        targets.append(((own, at), (side, at), (cross, at - BLK), (side, ALL + at - BLK)))
    for group, source, places in zip(copies, (k, q, g, v), targets):
        for copy in group:
            copy.wait()
        cut(source, places)


def merge_kernel(cross, side, q, g, v):
    for target, at, rows in ((q, Q_AT, BLK + MASK), (g, G_AT, BLK), (v, V_AT, BLK)):
        target[0] = cross[:, at - BLK : at - BLK + rows]
        target[1] = side[:, ALL + at - BLK : ALL + at - BLK + rows]


def stage_kernel(at, own, side, two, three, local, first, second):
    me = member()
    core = lax.rem(me, 2)
    for h in range(LOCAL):
        local[h, rows_of(me), :] = own[h, at : at + BLK]
        local[h, rows_of(jnp.bitwise_xor(me, 1)), :] = side[h, at : at + BLK]
        local[h, rows_of(jnp.bitwise_xor(me, 2)), :] = two[h]
        local[h, rows_of(jnp.bitwise_xor(me, 3)), :] = three[h]
    for h in range(LOCAL):
        first[h] = local[h, rows_of(REACH * (1 - core), REACH * BLK), :]
        second[h] = local[h, rows_of(REACH * core, REACH * BLK), :]


def stage_pair_kernel(at, own, side, pair, *outs):
    stage_kernel(at, own, side, pair.at[0], pair.at[1], *outs)


def nt(a, b):
    return lax.dot_general(a, b, (((1,), (1,)), ((), ())), preferred_element_type=f32)


def tn(a, b):
    return lax.dot_general(a, b, (((0,), (0,)), ((), ())), preferred_element_type=f32)


def nn(a, b):
    return lax.dot_general(a, b, (((1,), (0,)), ((), ())), preferred_element_type=f32)


def line_up(slots, h, local, first, second):
    core = lax.rem(member(), 2)
    top = REACH + TEAM
    slots[h, REACH * BLK : top * BLK, :] = local[h]
    slots[h, rows_of(core * top, REACH * BLK), :] = first[h]
    slots[h, rows_of((1 - core) * top, REACH * BLK), :] = second[h]


def key_sums(weights, rows, h, mine, ends, scale):
    for j in range(SLOTS):
        there = slice(j * BLK, (j + 1) * BLK)
        seen = slice(max(0, j - SPAN + 1) * BLK, (min(TEAM - 1, j) + 1) * BLK)
        term = nn(weights[h, there, seen], rows[h, seen, :])
        if scale is not None:
            term = term * scale
        if REACH <= j < REACH + TEAM:
            mine[h, (j - REACH) * BLK : (j - REACH + 1) * BLK, :] = term
        else:
            at = j if j < REACH else j - TEAM
            ends[at * BLK : (at + 1) * BLK, :] = term.astype(bf16)


def hand_ends(h, ends, first, second):
    core = lax.rem(member(), 2)
    first[h] = ends[rows_of(REACH * (1 - core), REACH * BLK), :]
    second[h] = ends[rows_of(REACH * core, REACH * BLK), :]


def probs_kernel(own, side, crossed, local, halo1, halo2, probs, ks, qs, bs):
    me = member()
    sources = ((own, Q_AT), (side, Q_AT), (crossed.at[0], 0), (crossed.at[1], 0))
    for h in range(LOCAL):
        line_up(ks, h, local, halo1, halo2)
        for step, (source, at) in enumerate(sources):
            position = jnp.bitwise_xor(me, step)
            qs[h, rows_of(position), :] = source[h, at : at + BLK]
            if h == 0:
                masks = pl.ds(pl.multiple_of(position * MASK, MASK), MASK)
                bs[masks, :] = source[h, at + BLK : at + BLK + MASK]
    for h in range(LOCAL):
        for pair in range(TEAM // 2):
            first = 2 * pair
            keys = ks[h, first * BLK : (first + SPAN + 1) * BLK, :]
            query = qs[h, first * BLK : (first + 2) * BLK, :]
            both = nt(keys, query)
            for n in range(2):
                i = first + n
                here = slice(i * BLK, (i + 1) * BLK)
                reach = slice(i * BLK, (i + SPAN) * BLK)
                bias = bs[i * MASK : (i + 1) * MASK, :].astype(f32)
                lanes = slice(n * BLK, (n + 1) * BLK)
                scores = jnp.concatenate(
                    [
                        both[(n + o) * BLK : (n + o + 1) * BLK, lanes] * (SCALE * LOG2E)
                        + bias[o : o + 1]
                        for o in range(SPAN)
                    ],
                    axis=0,
                )
                highest = jnp.max(scores, axis=0, keepdims=True)
                weights = jnp.exp2(scores - highest)
                scaled = weights * (1.0 / jnp.sum(weights, axis=0, keepdims=True))
                probs[h, reach, here] = scaled.astype(bf16)


def values_kernel(probs, own, side, crossed, gs, dv_own, dv1, dv2, ends):
    me = member()
    sources = ((own, G_AT), (side, G_AT), (crossed.at[0], 0), (crossed.at[1], 0))
    for h in range(LOCAL):
        for step, (source, at) in enumerate(sources):
            gs[h, rows_of(jnp.bitwise_xor(me, step)), :] = source[h, at : at + BLK]
        key_sums(probs, gs, h, dv_own, ends, None)
        hand_ends(h, ends, dv1, dv2)


def scores_kernel(probs, qs, gs, local, halo1, halo2, ss, dk_own, dk1, dk2, vs, ends):
    for h in range(LOCAL):
        line_up(vs, h, local, halo1, halo2)
        for pair in range(TEAM // 2):
            first = 2 * pair
            values = vs[h, first * BLK : (first + SPAN + 1) * BLK, :]
            grad = gs[h, first * BLK : (first + 2) * BLK, :]
            both = nt(values, grad)
            for n in range(2):
                i = first + n
                here = slice(i * BLK, (i + 1) * BLK)
                reach = slice(i * BLK, (i + SPAN) * BLK)
                grad_probs = both[n * BLK : (n + SPAN) * BLK, n * BLK : (n + 1) * BLK]
                weights = probs[h, reach, here].astype(f32)
                delta = jnp.sum(weights * grad_probs, axis=0, keepdims=True)
                ss[h, reach, here] = (weights * (grad_probs - delta)).astype(bf16)
        key_sums(ss, qs, h, dk_own, ends, SCALE)
        hand_ends(h, ends, dk1, dk2)


def queries_kernel(ss, ks, dq0, dq1, dq23, dqs):
    me = member()
    for h in range(LOCAL):
        for i in range(TEAM):
            here = slice(i * BLK, (i + 1) * BLK)
            reach = slice(i * BLK, (i + SPAN) * BLK)
            dqs[here, :] = (tn(ss[h, reach, here], ks[h, reach, :]) * SCALE).astype(bf16)
        for step, target in enumerate((dq0, dq1, dq23.at[0], dq23.at[1])):
            target[h] = dqs[rows_of(jnp.bitwise_xor(me, step)), :]


def total_kernel(mine, ring1, ring2, *outs):
    me = member()
    core = lax.rem(me, 2)
    for step in range(TEAM):
        block = jnp.bitwise_xor(me, step)
        use1 = block // REACH == core
        at = rows_of(lax.rem(block, REACH))
        for h in range(LOCAL):
            term = jnp.where(use1, ring1[h, at, :].astype(f32), ring2[h, at, :].astype(f32))
            outs[step][h] = (mine[h, rows_of(block), :] + term).astype(bf16)


def total_pairs_kernel(mine, ring1, ring2, stay, give):
    total_kernel(mine, ring1, ring2, stay.at[0], give.at[0], stay.at[1], give.at[1])


def join_kernel(stay, got, out):
    out[0] = stay[1]
    out[1] = got[1]


def gather_kernel(in0, in1, in2, in3, groups):
    me = member()
    for step, source in enumerate((in0, in1, in2, in3)):
        groups[jnp.bitwise_xor(me, step)] = source[...]


def write_out(parts, out, out_hbm, sems, wanted=None):
    copies = pieces(out, out_hbm, sems)
    count = BLK // len(copies)
    for n, copy in enumerate(copies):
        rows = slice(n * count, (n + 1) * count)
        for group, source in parts:
            for h in range(LOCAL):
                value = source[h, rows]
                if wanted is not None:
                    value = jnp.where(wanted, value, jnp.zeros_like(value))
                out[0, rows, head_columns(group, h)] = value
        copy.start()
    for copy in copies:
        copy.wait()


def unpack_kernel(in0, in1, in2, in3, out_hbm, out, sems):
    me = member()
    sources = (in0, in1, in2, in3)
    parts = [(jnp.bitwise_xor(me, step), source) for step, source in enumerate(sources)]
    write_out(parts, out, out_hbm, sems)


def unpack_joined_kernel(stay, got, crossed, *rest):
    unpack_kernel(stay.at[0], got.at[0], crossed.at[0], crossed.at[1], *rest)


def unpack_turned_kernel(dq0, dq1, crossed, turned, *rest):
    unpack_kernel(dq0, dq1, crossed.at[0], turned.at[1], *rest)


def unpack_passed_kernel(groups, out_hbm, out, sems):
    wanted = lax.axis_index("section") < lax.axis_size("section") - 1
    parts = [(group, groups.at[group]) for group in range(TEAM)]
    write_out(parts, out, out_hbm, sems, wanted)


def struct(*shape, dtype=bf16):
    return jax.ShapeDtypeStruct(shape, dtype)


HBM = pltpu.HBM
CUTS = 4


def call(kernel, name, outs, scratch=(), space=pltpu.VMEM, to=pltpu.VMEM):
    def run(*args):
        return pl.pallas_call(
            kernel,
            out_shape=jax.tree.map(lambda out: to(out.shape, out.dtype), outs),
            in_specs=[pl.BlockSpec(memory_space=space)] * len(args),
            out_specs=jax.tree.map(lambda _: pl.BlockSpec(memory_space=to), outs),
            scratch_shapes=scratch,
            compiler_params=pltpu.CompilerParams(vmem_limit_bytes=24 * 1024 * 1024),
            name=name,
        )(*(pltpu.with_memory_space_constraint(arg, space) for arg in args))

    return run


def after(array, *others):
    return lax.optimization_barrier((array, *others))[0]


def shards(query_rows, key_rows, value_rows, grad_output, block_lists):
    ctx = lax.axis_size("ctx")
    layers = ctx // TEAM
    width = query_rows.shape[2]

    def swap(array, step):
        return lax.ppermute(array, "ctx", [(i, i ^ step) for i in range(ctx)])

    def ring(array, flip):
        pairs = []
        for i in range(ctx):
            layer, up = i // TEAM, (i % 2) == flip
            inside = layer < layers - 1 if up else layer > 0
            pairs.append((i, (i + TEAM if up else i - TEAM) if inside else i ^ 1))
        return lax.ppermute(array, "ctx", pairs)

    part = struct(LOCAL, BLK, DH)
    pair = struct(2, LOCAL, BLK, DH)
    team = struct(LOCAL, TEAM * BLK, DH)
    ends = struct(LOCAL, REACH * BLK, DH)
    slots = struct(LOCAL, SLOTS * BLK, DH)
    square = struct(LOCAL, SLOTS * BLK, TEAM * BLK)
    kept = struct(LOCAL, TEAM * BLK, DH, dtype=f32)
    rows_in = pltpu.VMEM((1, BLK, width), bf16)
    ends_in = pltpu.VMEM((2 * REACH * BLK, DH), bf16)

    own, side, k2, k3, cross = call(
        pack_kernel,
        "pack",
        (struct(LOCAL, ALL, DH), struct(LOCAL, ALL + REST, DH), part, part, struct(LOCAL, REST, DH)),
        [pltpu.SMEM(block_lists.shape, jnp.int32), pltpu.SemaphoreType.DMA]
        + [rows_in] * 4
        + [pltpu.SemaphoreType.DMA((4, CUTS))],
        HBM,
    )(key_rows, query_rows, grad_output, value_rows, block_lists)
    k2 = swap(k2, 2)
    k3 = swap(k3, 3)
    side = swap(side, 1)
    q23, g23, v23 = call(
        merge_kernel, "merge", (struct(2, LOCAL, BLK + MASK, DH), pair, pair)
    )(cross, side)

    def stage(kernel, *blocks):
        local, first, second = call(kernel, "stage", (team, ends, ends))(*blocks)
        return local, ring(first, 0), ring(second, 1)

    k_local, k_halo1, k_halo2 = stage(functools.partial(stage_kernel, K_AT), own, side, k2, k3)
    q23 = swap(q23, 2)
    g23 = swap(after(g23, k2, k3), 2)
    v23 = swap(v23, 2)
    v_local, v_halo1, v_halo2 = stage(functools.partial(stage_pair_kernel, V_AT), own, side, v23)
    probs, ks, qs = call(
        probs_kernel, "probs", (square, slots, team), [pltpu.VMEM((TEAM * MASK, DH), bf16)]
    )(own, side, q23, k_local, k_halo1, k_halo2)
    g23 = after(g23, v_halo1, v_halo2)
    gs, dv_own, dv1, dv2 = call(values_kernel, "values", (team, kept, ends, ends), [ends_in])(
        probs, own, side, g23
    )

    def total(kernel, outs, mine, first, second):
        return call(kernel, "total", outs)(mine, ring(first, 0), ring(second, 1))

    def unpack(kernel, *parts):
        out = struct(1, BLK, width)
        sems = pltpu.SemaphoreType.DMA((CUTS,))
        return call(kernel, "unpack", out, [rows_in, sems], to=HBM)(*parts)

    ss, dk_own, dk1, dk2 = call(
        scores_kernel,
        "scores",
        (square, kept, ends, ends),
        [pltpu.VMEM((LOCAL, SLOTS * BLK, DH), bf16), ends_in],
    )(probs, qs, gs, v_local, v_halo1, v_halo2)
    dv = total(total_kernel, (part,) * 4, dv_own, dv1, dv2)
    dv_first = dv[0]
    dv = [dv[0]] + [swap(dv[step], step) for step in range(1, TEAM)]
    late = call(gather_kernel, "gather", struct(TEAM, LOCAL, BLK, DH))(*dv)
    sections = lax.axis_size("section")
    passed = lax.ppermute(late, "section", [(s, (s - 1) % sections) for s in range(sections)])
    dq0, dq1, dq23 = call(
        queries_kernel, "queries", (part, part, pair), [pltpu.VMEM((TEAM * BLK, DH), bf16)]
    )(ss, ks)
    dq23 = after(dq23, dv_first)
    dq23 = swap(dq23, 2)
    dk1 = after(dk1, dq0)
    dk2 = after(dk2, dq0)
    stay, give = total(total_pairs_kernel, (pair, pair), dk_own, dk1, dk2)
    got = swap(give, 1)
    joined = call(join_kernel, "join", pair)(after(stay, late), got)
    crossed = swap(joined, 2)
    dv[0] = after(dv[0], joined)
    grad_value = unpack(unpack_kernel, *dv)
    dq23 = after(dq23, got)
    grad_query = unpack(unpack_turned_kernel, dq0, swap(dq1, 1), dq23, swap(dq23, 1))
    grad_key = unpack(unpack_joined_kernel, stay, got, crossed)
    passed = after(passed, grad_key)
    handoff = unpack(unpack_passed_kernel, passed)
    return (grad_query, grad_key, grad_value, handoff)


def solution(mesh):
    wide = P("section", "ctx", None)
    return jax.shard_map(
        shards,
        mesh=mesh,
        in_specs=(wide, wide, wide, wide, P("ctx", None)),
        out_specs=(wide,) * 4,
        check_vma=False,
    )
```

```python
import functools

import jax
import jax.numpy as jnp
from jax import lax
from jax.experimental import pallas as pl
from jax.experimental.pallas import tpu as pltpu
from jax.sharding import PartitionSpec as P

H = 12
DH = 128
BLK = 128
REACH = 2
TEAM = 4
LOCAL = H // TEAM
SPAN = 2 * REACH + 1
SLOTS = TEAM + 2 * REACH
SCALE = DH ** (-0.5)
LOG2E = 1.4426950408889634
OFF = -1e30
MASK = 16
K_AT, Q_AT, M_AT, G_AT, V_AT = 0, BLK, 2 * BLK, 2 * BLK + MASK, 3 * BLK + MASK
ALL = 4 * BLK + MASK
REST = ALL - BLK

bf16 = jnp.bfloat16
f32 = jnp.float32


def member():
    return lax.rem(lax.axis_index("ctx"), TEAM)


def rows_of(index, count=BLK):
    return pl.ds(pl.multiple_of(index * BLK, BLK), count)


def head_columns(group, h):
    return pl.ds(pl.multiple_of(group * (LOCAL * DH) + h * DH, DH), DH)


def pieces(source, target, sems):
    count = sems.shape[0]
    rows = BLK // count
    return [
        pltpu.make_async_copy(
            source.at[0, n * rows : (n + 1) * rows], target.at[0, n * rows : (n + 1) * rows], sems.at[n]
        )
        for n in range(count)
    ]


def cut(source, targets):
    me = member()
    for step, (target, base) in enumerate(targets):
        group = jnp.bitwise_xor(me, step)
        for h in range(LOCAL):
            target[h, base : base + BLK, :] = source[0, :, head_columns(group, h)]


def pack_kernel(
    k_hbm, q_hbm, g_hbm, v_hbm, lists_hbm, own, side, k2, k3, cross, lists, lists_sem, k, q, g, v, sems
):
    copies = [
        pieces(source, target, sems.at[n])
        for n, (source, target) in enumerate(((k_hbm, k), (q_hbm, q), (g_hbm, g), (v_hbm, v)))
    ]
    lists_copy = pltpu.make_async_copy(lists_hbm, lists, lists_sem)
    lists_copy.start()
    for group in copies:
        for copy in group:
            copy.start()
    block = lax.axis_index("ctx")
    lists_copy.wait()
    row = lax.broadcasted_iota(jnp.int32, (MASK, DH), 0)
    mask = jnp.full((MASK, DH), OFF, f32)
    for o in range(SPAN):
        wanted = jnp.int32(0)
        for n in range(lists.shape[1]):
            entry = lists[0, n]
            hit = (entry >= 0) & (entry == block + (o - REACH))
            wanted = jnp.maximum(wanted, hit.astype(jnp.int32))
        level = jnp.where(wanted > 0, 0.0, OFF).astype(f32)
        mask = jnp.where(row == o, level, mask)
    mask = mask.astype(bf16)
    for target, at in ((own, M_AT), (side, M_AT), (side, ALL + M_AT - BLK), (cross, M_AT - BLK)):
        for h in range(LOCAL):
            target[h, at : at + MASK, :] = mask
    targets = [((own, K_AT), (side, K_AT), (k2, 0), (k3, 0))]
    for at in (Q_AT, G_AT, V_AT):
        targets.append(((own, at), (side, at), (cross, at - BLK), (side, ALL + at - BLK)))
    for group, source, places in zip(copies, (k, q, g, v), targets):
        for copy in group:
            copy.wait()
        cut(source, places)


def merge_kernel(cross, side, q, g, v):
    for target, at, rows in ((q, Q_AT, BLK + MASK), (g, G_AT, BLK), (v, V_AT, BLK)):
        target[0] = cross[:, at - BLK : at - BLK + rows]
        target[1] = side[:, ALL + at - BLK : ALL + at - BLK + rows]


def stage_kernel(at, own, side, two, three, local, first, second):
    me = member()
    core = lax.rem(me, 2)
    for h in range(LOCAL):
        local[h, rows_of(me), :] = own[h, at : at + BLK]
        local[h, rows_of(jnp.bitwise_xor(me, 1)), :] = side[h, at : at + BLK]
        local[h, rows_of(jnp.bitwise_xor(me, 2)), :] = two[h]
        local[h, rows_of(jnp.bitwise_xor(me, 3)), :] = three[h]
    for h in range(LOCAL):
        first[h] = local[h, rows_of(REACH * (1 - core), REACH * BLK), :]
        second[h] = local[h, rows_of(REACH * core, REACH * BLK), :]


def stage_pair_kernel(at, own, side, pair, *outs):
    stage_kernel(at, own, side, pair.at[0], pair.at[1], *outs)


def nt(a, b):
    return lax.dot_general(a, b, (((1,), (1,)), ((), ())), preferred_element_type=f32)


def tn(a, b):
    return lax.dot_general(a, b, (((0,), (0,)), ((), ())), preferred_element_type=f32)


def nn(a, b):
    return lax.dot_general(a, b, (((1,), (0,)), ((), ())), preferred_element_type=f32)


def line_up(slots, h, local, first, second):
    core = lax.rem(member(), 2)
    top = REACH + TEAM
    slots[h, REACH * BLK : top * BLK, :] = local[h]
    slots[h, rows_of(core * top, REACH * BLK), :] = first[h]
    slots[h, rows_of((1 - core) * top, REACH * BLK), :] = second[h]


def key_sums(weights, rows, h, mine, ends, scale):
    for j in range(SLOTS):
        there = slice(j * BLK, (j + 1) * BLK)
        seen = slice(max(0, j - SPAN + 1) * BLK, (min(TEAM - 1, j) + 1) * BLK)
        term = nn(weights[h, there, seen], rows[h, seen, :])
        if scale is not None:
            term = term * scale
        if REACH <= j < REACH + TEAM:
            mine[h, (j - REACH) * BLK : (j - REACH + 1) * BLK, :] = term
        else:
            at = j if j < REACH else j - TEAM
            ends[at * BLK : (at + 1) * BLK, :] = term.astype(bf16)


def hand_ends(h, ends, first, second):
    core = lax.rem(member(), 2)
    first[h] = ends[rows_of(REACH * (1 - core), REACH * BLK), :]
    second[h] = ends[rows_of(REACH * core, REACH * BLK), :]


def probs_kernel(own, side, crossed, local, halo1, halo2, probs, ks, qs, bs):
    me = member()
    sources = ((own, Q_AT), (side, Q_AT), (crossed.at[0], 0), (crossed.at[1], 0))
    for h in range(LOCAL):
        line_up(ks, h, local, halo1, halo2)
        for step, (source, at) in enumerate(sources):
            position = jnp.bitwise_xor(me, step)
            qs[h, rows_of(position), :] = source[h, at : at + BLK]
            if h == 0:
                masks = pl.ds(pl.multiple_of(position * MASK, MASK), MASK)
                bs[masks, :] = source[h, at + BLK : at + BLK + MASK]
    for h in range(LOCAL):
        for pair in range(TEAM // 2):
            first = 2 * pair
            keys = ks[h, first * BLK : (first + SPAN + 1) * BLK, :]
            query = qs[h, first * BLK : (first + 2) * BLK, :]
            both = nt(keys, query)
            for n in range(2):
                i = first + n
                here = slice(i * BLK, (i + 1) * BLK)
                reach = slice(i * BLK, (i + SPAN) * BLK)
                bias = bs[i * MASK : (i + 1) * MASK, :].astype(f32)
                lanes = slice(n * BLK, (n + 1) * BLK)
                scores = jnp.concatenate(
                    [
                        both[(n + o) * BLK : (n + o + 1) * BLK, lanes] * (SCALE * LOG2E)
                        + bias[o : o + 1]
                        for o in range(SPAN)
                    ],
                    axis=0,
                )
                highest = jnp.max(scores, axis=0, keepdims=True)
                weights = jnp.exp2(scores - highest)
                scaled = weights * (1.0 / jnp.sum(weights, axis=0, keepdims=True))
                probs[h, reach, here] = scaled.astype(bf16)


def values_kernel(probs, own, side, crossed, gs, dv_own, dv1, dv2, ends):
    me = member()
    sources = ((own, G_AT), (side, G_AT), (crossed.at[0], 0), (crossed.at[1], 0))
    for h in range(LOCAL):
        for step, (source, at) in enumerate(sources):
            gs[h, rows_of(jnp.bitwise_xor(me, step)), :] = source[h, at : at + BLK]
        key_sums(probs, gs, h, dv_own, ends, None)
        hand_ends(h, ends, dv1, dv2)


def scores_kernel(probs, qs, gs, local, halo1, halo2, ss, dk_own, dk1, dk2, vs, ends):
    for h in range(LOCAL):
        line_up(vs, h, local, halo1, halo2)
        for pair in range(TEAM // 2):
            first = 2 * pair
            values = vs[h, first * BLK : (first + SPAN + 1) * BLK, :]
            grad = gs[h, first * BLK : (first + 2) * BLK, :]
            both = nt(values, grad)
            for n in range(2):
                i = first + n
                here = slice(i * BLK, (i + 1) * BLK)
                reach = slice(i * BLK, (i + SPAN) * BLK)
                grad_probs = both[n * BLK : (n + SPAN) * BLK, n * BLK : (n + 1) * BLK]
                weights = probs[h, reach, here].astype(f32)
                delta = jnp.sum(weights * grad_probs, axis=0, keepdims=True)
                ss[h, reach, here] = (weights * (grad_probs - delta)).astype(bf16)
        key_sums(ss, qs, h, dk_own, ends, SCALE)
        hand_ends(h, ends, dk1, dk2)


def queries_kernel(ss, ks, dq0, dq1, dq23, dqs):
    me = member()
    for h in range(LOCAL):
        for i in range(TEAM):
            here = slice(i * BLK, (i + 1) * BLK)
            reach = slice(i * BLK, (i + SPAN) * BLK)
            dqs[here, :] = (tn(ss[h, reach, here], ks[h, reach, :]) * SCALE).astype(bf16)
        for step, target in enumerate((dq0, dq1, dq23.at[0], dq23.at[1])):
            target[h] = dqs[rows_of(jnp.bitwise_xor(me, step)), :]


def total_kernel(mine, ring1, ring2, *outs):
    me = member()
    core = lax.rem(me, 2)
    for step in range(TEAM):
        block = jnp.bitwise_xor(me, step)
        use1 = block // REACH == core
        at = rows_of(lax.rem(block, REACH))
        for h in range(LOCAL):
            term = jnp.where(use1, ring1[h, at, :].astype(f32), ring2[h, at, :].astype(f32))
            outs[step][h] = (mine[h, rows_of(block), :] + term).astype(bf16)


def total_pairs_kernel(mine, ring1, ring2, stay, give):
    total_kernel(mine, ring1, ring2, stay.at[0], give.at[0], stay.at[1], give.at[1])


def join_kernel(stay, got, out):
    out[0] = stay[1]
    out[1] = got[1]


def gather_kernel(in0, in1, in2, in3, groups):
    me = member()
    for step, source in enumerate((in0, in1, in2, in3)):
        groups[jnp.bitwise_xor(me, step)] = source[...]


def fill_out(parts, out, out_hbm, sems, wanted=None):
    copies = pieces(out, out_hbm, sems)
    count = BLK // len(copies)
    for n, copy in enumerate(copies):
        rows = slice(n * count, (n + 1) * count)
        for group, source in parts:
            for h in range(LOCAL):
                value = source[h, rows]
                if wanted is not None:
                    value = jnp.where(wanted, value, jnp.zeros_like(value))
                out[0, rows, head_columns(group, h)] = value
        copy.start()
    return copies


def by_step(*sources):
    me = member()
    return [(jnp.bitwise_xor(me, step), source) for step, source in enumerate(sources)]


def unpack_kernel(in0, in1, in2, in3, out_hbm, out, sems):
    for copy in fill_out(by_step(in0, in1, in2, in3), out, out_hbm, sems):
        copy.wait()


def unpack_last_kernel(
    dq0, dq1, dq23, turned, stay, got, crossed, groups,
    dq_hbm, dk_hbm, passed_hbm, dq, dk, passed, sems,
):
    copies = fill_out(by_step(dq0, dq1, dq23.at[0], turned.at[1]), dq, dq_hbm, sems.at[0])
    sources = by_step(stay.at[0], got.at[0], crossed.at[0], crossed.at[1])
    copies += fill_out(sources, dk, dk_hbm, sems.at[1])
    wanted = lax.axis_index("section") < lax.axis_size("section") - 1
    sources = [(group, groups.at[group]) for group in range(TEAM)]
    copies += fill_out(sources, passed, passed_hbm, sems.at[2], wanted)
    for copy in copies:
        copy.wait()


def struct(*shape, dtype=bf16):
    return jax.ShapeDtypeStruct(shape, dtype)


HBM = pltpu.HBM
CUTS = 4


def call(kernel, name, outs, scratch=(), space=pltpu.VMEM, to=pltpu.VMEM):
    def run(*args):
        return pl.pallas_call(
            kernel,
            out_shape=jax.tree.map(lambda out: to(out.shape, out.dtype), outs),
            in_specs=[pl.BlockSpec(memory_space=space)] * len(args),
            out_specs=jax.tree.map(lambda _: pl.BlockSpec(memory_space=to), outs),
            scratch_shapes=scratch,
            compiler_params=pltpu.CompilerParams(vmem_limit_bytes=24 * 1024 * 1024),
            name=name,
        )(*(pltpu.with_memory_space_constraint(arg, space) for arg in args))

    return run


def after(array, *others):
    return lax.optimization_barrier((array, *others))[0]


def shards(query_rows, key_rows, value_rows, grad_output, block_lists):
    ctx = lax.axis_size("ctx")
    layers = ctx // TEAM
    width = query_rows.shape[2]

    def swap(array, step):
        return lax.ppermute(array, "ctx", [(i, i ^ step) for i in range(ctx)])

    def ring(array, flip):
        pairs = []
        for i in range(ctx):
            layer, up = i // TEAM, (i % 2) == flip
            inside = layer < layers - 1 if up else layer > 0
            pairs.append((i, (i + TEAM if up else i - TEAM) if inside else i ^ 1))
        return lax.ppermute(array, "ctx", pairs)

    part = struct(LOCAL, BLK, DH)
    pair = struct(2, LOCAL, BLK, DH)
    team = struct(LOCAL, TEAM * BLK, DH)
    ends = struct(LOCAL, REACH * BLK, DH)
    slots = struct(LOCAL, SLOTS * BLK, DH)
    square = struct(LOCAL, SLOTS * BLK, TEAM * BLK)
    kept = struct(LOCAL, TEAM * BLK, DH, dtype=f32)
    rows_in = pltpu.VMEM((1, BLK, width), bf16)
    ends_in = pltpu.VMEM((2 * REACH * BLK, DH), bf16)

    own, side, k2, k3, cross = call(
        pack_kernel,
        "pack",
        (struct(LOCAL, ALL, DH), struct(LOCAL, ALL + REST, DH), part, part, struct(LOCAL, REST, DH)),
        [pltpu.SMEM(block_lists.shape, jnp.int32), pltpu.SemaphoreType.DMA]
        + [rows_in] * 4
        + [pltpu.SemaphoreType.DMA((4, CUTS))],
        HBM,
    )(key_rows, query_rows, grad_output, value_rows, block_lists)
    k2 = swap(k2, 2)
    k3 = swap(k3, 3)
    side = swap(side, 1)
    q23, g23, v23 = call(
        merge_kernel, "merge", (struct(2, LOCAL, BLK + MASK, DH), pair, pair)
    )(cross, side)

    def stage(kernel, *blocks):
        local, first, second = call(kernel, "stage", (team, ends, ends))(*blocks)
        return local, ring(first, 0), ring(second, 1)

    k_local, k_halo1, k_halo2 = stage(functools.partial(stage_kernel, K_AT), own, side, k2, k3)
    q23 = swap(q23, 2)
    g23 = swap(after(g23, k2, k3), 2)
    v23 = swap(v23, 2)
    v_local, v_halo1, v_halo2 = stage(functools.partial(stage_pair_kernel, V_AT), own, side, v23)
    probs, ks, qs = call(
        probs_kernel, "probs", (square, slots, team), [pltpu.VMEM((TEAM * MASK, DH), bf16)]
    )(own, side, q23, k_local, k_halo1, k_halo2)
    g23 = after(g23, v_halo1, v_halo2)
    gs, dv_own, dv1, dv2 = call(values_kernel, "values", (team, kept, ends, ends), [ends_in])(
        probs, own, side, g23
    )

    def total(kernel, outs, mine, first, second):
        return call(kernel, "total", outs)(mine, ring(first, 0), ring(second, 1))

    def unpack(kernel, *parts):
        out = struct(1, BLK, width)
        sems = pltpu.SemaphoreType.DMA((CUTS,))
        return call(kernel, "unpack", out, [rows_in, sems], to=HBM)(*parts)

    ss, dk_own, dk1, dk2 = call(
        scores_kernel,
        "scores",
        (square, kept, ends, ends),
        [pltpu.VMEM((LOCAL, SLOTS * BLK, DH), bf16), ends_in],
    )(probs, qs, gs, v_local, v_halo1, v_halo2)
    dv = total(total_kernel, (part,) * 4, dv_own, dv1, dv2)
    dv_first = dv[0]
    dv = [dv[0]] + [swap(dv[step], step) for step in range(1, TEAM)]
    late = call(gather_kernel, "gather", struct(TEAM, LOCAL, BLK, DH))(*dv)
    sections = lax.axis_size("section")
    passed = lax.ppermute(late, "section", [(s, (s - 1) % sections) for s in range(sections)])
    dq0, dq1, dq23 = call(
        queries_kernel, "queries", (part, part, pair), [pltpu.VMEM((TEAM * BLK, DH), bf16)]
    )(ss, ks)
    dq23 = after(dq23, dv_first)
    dq23 = swap(dq23, 2)
    dk1 = after(dk1, dq0)
    dk2 = after(dk2, dq0)
    stay, give = total(total_pairs_kernel, (pair, pair), dk_own, dk1, dk2)
    got = swap(give, 1)
    joined = call(join_kernel, "join", pair)(after(stay, late), got)
    crossed = swap(joined, 2)
    dv[0] = after(dv[0], joined)
    grad_value = unpack(unpack_kernel, *dv)
    dq23 = after(dq23, got)
    out = struct(1, BLK, width)
    grad_query, grad_key, handoff = call(
        unpack_last_kernel,
        "unpack",
        (out,) * 3,
        [rows_in] * 3 + [pltpu.SemaphoreType.DMA((3, CUTS))],
        to=HBM,
    )(dq0, swap(dq1, 1), dq23, swap(dq23, 1), stay, got, crossed, passed)
    return (grad_query, grad_key, grad_value, handoff)


def solution(mesh):
    wide = P("section", "ctx", None)
    return jax.shard_map(
        shards,
        mesh=mesh,
        in_specs=(wide, wide, wide, wide, P("ctx", None)),
        out_specs=(wide,) * 4,
        check_vma=False,
    )
```

```python
import functools

import jax
import jax.numpy as jnp
from jax import lax
from jax.experimental import pallas as pl
from jax.experimental.pallas import tpu as pltpu
from jax.sharding import PartitionSpec as P

H = 12
DH = 128
BLK = 128
REACH = 2
TEAM = 4
LOCAL = H // TEAM
SPAN = 2 * REACH + 1
SLOTS = TEAM + 2 * REACH
SCALE = DH ** (-0.5)
LOG2E = 1.4426950408889634
OFF = -1e30
MASK = 16
K_AT, Q_AT, M_AT, G_AT, V_AT = 0, BLK, 2 * BLK, 2 * BLK + MASK, 3 * BLK + MASK
ALL = 4 * BLK + MASK
REST = ALL - BLK

bf16 = jnp.bfloat16
f32 = jnp.float32


def member():
    return lax.rem(lax.axis_index("ctx"), TEAM)


def rows_of(index, count=BLK):
    return pl.ds(pl.multiple_of(index * BLK, BLK), count)


def head_columns(group, h):
    return pl.ds(pl.multiple_of(group * (LOCAL * DH) + h * DH, DH), DH)


def pieces(source, target, sems):
    count = sems.shape[0]
    rows = BLK // count
    return [
        pltpu.make_async_copy(
            source.at[0, n * rows : (n + 1) * rows], target.at[0, n * rows : (n + 1) * rows], sems.at[n]
        )
        for n in range(count)
    ]


def cut(source, targets):
    me = member()
    for step, (target, base) in enumerate(targets):
        group = jnp.bitwise_xor(me, step)
        for h in range(LOCAL):
            target[h, base : base + BLK, :] = source[0, :, head_columns(group, h)]


def pack_kernel(
    k_hbm, q_hbm, g_hbm, v_hbm, lists_hbm, own, side, k2, k3, cross, lists, lists_sem, k, q, g, v, sems
):
    copies = [
        pieces(source, target, sems.at[n])
        for n, (source, target) in enumerate(((k_hbm, k), (q_hbm, q), (g_hbm, g), (v_hbm, v)))
    ]
    lists_copy = pltpu.make_async_copy(lists_hbm, lists, lists_sem)
    lists_copy.start()
    for group in copies:
        for copy in group:
            copy.start()
    block = lax.axis_index("ctx")
    lists_copy.wait()
    row = lax.broadcasted_iota(jnp.int32, (MASK, DH), 0)
    mask = jnp.full((MASK, DH), OFF, f32)
    for o in range(SPAN):
        wanted = jnp.int32(0)
        for n in range(lists.shape[1]):
            entry = lists[0, n]
            hit = (entry >= 0) & (entry == block + (o - REACH))
            wanted = jnp.maximum(wanted, hit.astype(jnp.int32))
        level = jnp.where(wanted > 0, 0.0, OFF).astype(f32)
        mask = jnp.where(row == o, level, mask)
    mask = mask.astype(bf16)
    for target, at in ((own, M_AT), (side, M_AT), (side, ALL + M_AT - BLK), (cross, M_AT - BLK)):
        for h in range(LOCAL):
            target[h, at : at + MASK, :] = mask
    targets = [((own, K_AT), (side, K_AT), (k2, 0), (k3, 0))]
    for at in (Q_AT, G_AT, V_AT):
        targets.append(((own, at), (side, at), (cross, at - BLK), (side, ALL + at - BLK)))
    for group, source, places in zip(copies, (k, q, g, v), targets):
        for copy in group:
            copy.wait()
        cut(source, places)


def merge_kernel(cross, side, q, g, v):
    for target, at, rows in ((q, Q_AT, BLK + MASK), (g, G_AT, BLK), (v, V_AT, BLK)):
        target[0] = cross[:, at - BLK : at - BLK + rows]
        target[1] = side[:, ALL + at - BLK : ALL + at - BLK + rows]


def stage_kernel(at, own, side, two, three, local, first, second):
    me = member()
    core = lax.rem(me, 2)
    for h in range(LOCAL):
        local[h, rows_of(me), :] = own[h, at : at + BLK]
        local[h, rows_of(jnp.bitwise_xor(me, 1)), :] = side[h, at : at + BLK]
        local[h, rows_of(jnp.bitwise_xor(me, 2)), :] = two[h]
        local[h, rows_of(jnp.bitwise_xor(me, 3)), :] = three[h]
    for h in range(LOCAL):
        first[h] = local[h, rows_of(REACH * (1 - core), REACH * BLK), :]
        second[h] = local[h, rows_of(REACH * core, REACH * BLK), :]


def stage_pair_kernel(at, own, side, pair, *outs):
    stage_kernel(at, own, side, pair.at[0], pair.at[1], *outs)


def nt(a, b):
    return lax.dot_general(a, b, (((1,), (1,)), ((), ())), preferred_element_type=f32)


def tn(a, b):
    return lax.dot_general(a, b, (((0,), (0,)), ((), ())), preferred_element_type=f32)


def nn(a, b):
    return lax.dot_general(a, b, (((1,), (0,)), ((), ())), preferred_element_type=f32)


def line_up(slots, h, local, first, second):
    core = lax.rem(member(), 2)
    top = REACH + TEAM
    slots[h, REACH * BLK : top * BLK, :] = local[h]
    slots[h, rows_of(core * top, REACH * BLK), :] = first[h]
    slots[h, rows_of((1 - core) * top, REACH * BLK), :] = second[h]


def key_sums(weights, rows, h, mine, ends, scale):
    for j in range(SLOTS):
        there = slice(j * BLK, (j + 1) * BLK)
        seen = slice(max(0, j - SPAN + 1) * BLK, (min(TEAM - 1, j) + 1) * BLK)
        term = nn(weights[h, there, seen], rows[h, seen, :])
        if scale is not None:
            term = term * scale
        if REACH <= j < REACH + TEAM:
            mine[h, (j - REACH) * BLK : (j - REACH + 1) * BLK, :] = term
        else:
            at = j if j < REACH else j - TEAM
            ends[at * BLK : (at + 1) * BLK, :] = term.astype(bf16)


def hand_ends(h, ends, first, second):
    core = lax.rem(member(), 2)
    first[h] = ends[rows_of(REACH * (1 - core), REACH * BLK), :]
    second[h] = ends[rows_of(REACH * core, REACH * BLK), :]


def probs_kernel(own, side, crossed, local, halo1, halo2, probs, ks, qs, bs):
    me = member()
    sources = ((own, Q_AT), (side, Q_AT), (crossed.at[0], 0), (crossed.at[1], 0))
    for h in range(LOCAL):
        line_up(ks, h, local, halo1, halo2)
        for step, (source, at) in enumerate(sources):
            position = jnp.bitwise_xor(me, step)
            qs[h, rows_of(position), :] = source[h, at : at + BLK]
            if h == 0:
                masks = pl.ds(pl.multiple_of(position * MASK, MASK), MASK)
                bs[masks, :] = source[h, at + BLK : at + BLK + MASK]
    for h in range(LOCAL):
        for pair in range(TEAM // 2):
            first = 2 * pair
            keys = ks[h, first * BLK : (first + SPAN + 1) * BLK, :]
            query = qs[h, first * BLK : (first + 2) * BLK, :]
            both = nt(keys, query)
            for n in range(2):
                i = first + n
                here = slice(i * BLK, (i + 1) * BLK)
                reach = slice(i * BLK, (i + SPAN) * BLK)
                bias = bs[i * MASK : (i + 1) * MASK, :].astype(f32)
                lanes = slice(n * BLK, (n + 1) * BLK)
                scores = jnp.concatenate(
                    [
                        both[(n + o) * BLK : (n + o + 1) * BLK, lanes] * (SCALE * LOG2E)
                        + bias[o : o + 1]
                        for o in range(SPAN)
                    ],
                    axis=0,
                )
                highest = jnp.max(scores, axis=0, keepdims=True)
                weights = jnp.exp2(scores - highest)
                scaled = weights * (1.0 / jnp.sum(weights, axis=0, keepdims=True))
                probs[h, reach, here] = scaled.astype(bf16)


def values_kernel(probs, own, side, crossed, gs, dv_own, dv1, dv2, ends):
    me = member()
    sources = ((own, G_AT), (side, G_AT), (crossed.at[0], 0), (crossed.at[1], 0))
    for h in range(LOCAL):
        for step, (source, at) in enumerate(sources):
            gs[h, rows_of(jnp.bitwise_xor(me, step)), :] = source[h, at : at + BLK]
        key_sums(probs, gs, h, dv_own, ends, None)
        hand_ends(h, ends, dv1, dv2)


def scores_kernel(probs, qs, gs, local, halo1, halo2, ss, dk_own, dk1, dk2, vs, ends):
    for h in range(LOCAL):
        line_up(vs, h, local, halo1, halo2)
        for pair in range(TEAM // 2):
            first = 2 * pair
            values = vs[h, first * BLK : (first + SPAN + 1) * BLK, :]
            grad = gs[h, first * BLK : (first + 2) * BLK, :]
            both = nt(values, grad)
            for n in range(2):
                i = first + n
                here = slice(i * BLK, (i + 1) * BLK)
                reach = slice(i * BLK, (i + SPAN) * BLK)
                grad_probs = both[n * BLK : (n + SPAN) * BLK, n * BLK : (n + 1) * BLK]
                weights = probs[h, reach, here].astype(f32)
                delta = jnp.sum(weights * grad_probs, axis=0, keepdims=True)
                ss[h, reach, here] = (weights * (grad_probs - delta)).astype(bf16)
        key_sums(ss, qs, h, dk_own, ends, SCALE)
        hand_ends(h, ends, dk1, dk2)


def queries_kernel(ss, ks, dq0, dq1, dq23, dqs):
    me = member()
    for h in range(LOCAL):
        for i in range(TEAM):
            here = slice(i * BLK, (i + 1) * BLK)
            reach = slice(i * BLK, (i + SPAN) * BLK)
            dqs[here, :] = (tn(ss[h, reach, here], ks[h, reach, :]) * SCALE).astype(bf16)
        for step, target in enumerate((dq0, dq1, dq23.at[0], dq23.at[1])):
            target[h] = dqs[rows_of(jnp.bitwise_xor(me, step)), :]


def total_kernel(mine, ring1, ring2, *outs):
    me = member()
    core = lax.rem(me, 2)
    for step in range(TEAM):
        block = jnp.bitwise_xor(me, step)
        use1 = block // REACH == core
        at = rows_of(lax.rem(block, REACH))
        for h in range(LOCAL):
            term = jnp.where(use1, ring1[h, at, :].astype(f32), ring2[h, at, :].astype(f32))
            outs[step][h] = (mine[h, rows_of(block), :] + term).astype(bf16)


def total_pairs_kernel(mine, ring1, ring2, stay, give):
    total_kernel(mine, ring1, ring2, stay.at[0], give.at[0], stay.at[1], give.at[1])


def join_kernel(stay, got, out):
    out[0] = stay[1]
    out[1] = got[1]


def gather_kernel(in0, in1, in2, in3, groups):
    me = member()
    for step, source in enumerate((in0, in1, in2, in3)):
        groups[jnp.bitwise_xor(me, step)] = source[...]


def write_out(parts, out, out_hbm, sems, wanted=None):
    copies = pieces(out, out_hbm, sems)
    count = BLK // len(copies)
    for n, copy in enumerate(copies):
        rows = slice(n * count, (n + 1) * count)
        for group, source in parts:
            for h in range(LOCAL):
                value = source[h, rows]
                if wanted is not None:
                    value = jnp.where(wanted, value, jnp.zeros_like(value))
                out[0, rows, head_columns(group, h)] = value
        copy.start()
    for copy in copies:
        copy.wait()


def unpack_kernel(in0, in1, in2, in3, out_hbm, out, sems):
    me = member()
    sources = (in0, in1, in2, in3)
    parts = [(jnp.bitwise_xor(me, step), source) for step, source in enumerate(sources)]
    write_out(parts, out, out_hbm, sems)


def unpack_joined_kernel(stay, got, crossed, *rest):
    unpack_kernel(stay.at[0], got.at[0], crossed.at[0], crossed.at[1], *rest)


def unpack_turned_kernel(dq0, dq1, crossed, turned, *rest):
    unpack_kernel(dq0, dq1, crossed.at[0], turned.at[1], *rest)


def unpack_passed_kernel(groups, out_hbm, out, sems):
    wanted = lax.axis_index("section") < lax.axis_size("section") - 1
    parts = [(group, groups.at[group]) for group in range(TEAM)]
    write_out(parts, out, out_hbm, sems, wanted)


def struct(*shape, dtype=bf16):
    return jax.ShapeDtypeStruct(shape, dtype)


HBM = pltpu.HBM
CUTS = 8


def call(kernel, name, outs, scratch=(), space=pltpu.VMEM, to=pltpu.VMEM):
    def run(*args):
        return pl.pallas_call(
            kernel,
            out_shape=jax.tree.map(lambda out: to(out.shape, out.dtype), outs),
            in_specs=[pl.BlockSpec(memory_space=space)] * len(args),
            out_specs=jax.tree.map(lambda _: pl.BlockSpec(memory_space=to), outs),
            scratch_shapes=scratch,
            compiler_params=pltpu.CompilerParams(vmem_limit_bytes=24 * 1024 * 1024),
            name=name,
        )(*(pltpu.with_memory_space_constraint(arg, space) for arg in args))

    return run


def after(array, *others):
    return lax.optimization_barrier((array, *others))[0]


def shards(query_rows, key_rows, value_rows, grad_output, block_lists):
    ctx = lax.axis_size("ctx")
    layers = ctx // TEAM
    width = query_rows.shape[2]

    def swap(array, step):
        return lax.ppermute(array, "ctx", [(i, i ^ step) for i in range(ctx)])

    def ring(array, flip):
        pairs = []
        for i in range(ctx):
            layer, up = i // TEAM, (i % 2) == flip
            inside = layer < layers - 1 if up else layer > 0
            pairs.append((i, (i + TEAM if up else i - TEAM) if inside else i ^ 1))
        return lax.ppermute(array, "ctx", pairs)

    part = struct(LOCAL, BLK, DH)
    pair = struct(2, LOCAL, BLK, DH)
    team = struct(LOCAL, TEAM * BLK, DH)
    ends = struct(LOCAL, REACH * BLK, DH)
    slots = struct(LOCAL, SLOTS * BLK, DH)
    square = struct(LOCAL, SLOTS * BLK, TEAM * BLK)
    kept = struct(LOCAL, TEAM * BLK, DH, dtype=f32)
    rows_in = pltpu.VMEM((1, BLK, width), bf16)
    ends_in = pltpu.VMEM((2 * REACH * BLK, DH), bf16)

    own, side, k2, k3, cross = call(
        pack_kernel,
        "pack",
        (struct(LOCAL, ALL, DH), struct(LOCAL, ALL + REST, DH), part, part, struct(LOCAL, REST, DH)),
        [pltpu.SMEM(block_lists.shape, jnp.int32), pltpu.SemaphoreType.DMA]
        + [rows_in] * 4
        + [pltpu.SemaphoreType.DMA((4, CUTS))],
        HBM,
    )(key_rows, query_rows, grad_output, value_rows, block_lists)
    k2 = swap(k2, 2)
    k3 = swap(k3, 3)
    side = swap(side, 1)
    q23, g23, v23 = call(
        merge_kernel, "merge", (struct(2, LOCAL, BLK + MASK, DH), pair, pair)
    )(cross, side)

    def stage(kernel, *blocks):
        local, first, second = call(kernel, "stage", (team, ends, ends))(*blocks)
        return local, ring(first, 0), ring(second, 1)

    k_local, k_halo1, k_halo2 = stage(functools.partial(stage_kernel, K_AT), own, side, k2, k3)
    q23 = swap(q23, 2)
    g23 = swap(after(g23, k2, k3), 2)
    v23 = swap(v23, 2)
    v_local, v_halo1, v_halo2 = stage(functools.partial(stage_pair_kernel, V_AT), own, side, v23)
    probs, ks, qs = call(
        probs_kernel, "probs", (square, slots, team), [pltpu.VMEM((TEAM * MASK, DH), bf16)]
    )(own, side, q23, k_local, k_halo1, k_halo2)
    g23 = after(g23, v_halo1, v_halo2)
    gs, dv_own, dv1, dv2 = call(values_kernel, "values", (team, kept, ends, ends), [ends_in])(
        probs, own, side, g23
    )

    def total(kernel, outs, mine, first, second):
        return call(kernel, "total", outs)(mine, ring(first, 0), ring(second, 1))

    def unpack(kernel, *parts):
        out = struct(1, BLK, width)
        sems = pltpu.SemaphoreType.DMA((CUTS,))
        return call(kernel, "unpack", out, [rows_in, sems], to=HBM)(*parts)

    ss, dk_own, dk1, dk2 = call(
        scores_kernel,
        "scores",
        (square, kept, ends, ends),
        [pltpu.VMEM((LOCAL, SLOTS * BLK, DH), bf16), ends_in],
    )(probs, qs, gs, v_local, v_halo1, v_halo2)
    dv = total(total_kernel, (part,) * 4, dv_own, dv1, dv2)
    dv_first = dv[0]
    dv = [dv[0]] + [swap(dv[step], step) for step in range(1, TEAM)]
    late = call(gather_kernel, "gather", struct(TEAM, LOCAL, BLK, DH))(*dv)
    sections = lax.axis_size("section")
    passed = lax.ppermute(late, "section", [(s, (s - 1) % sections) for s in range(sections)])
    dq0, dq1, dq23 = call(
        queries_kernel, "queries", (part, part, pair), [pltpu.VMEM((TEAM * BLK, DH), bf16)]
    )(ss, ks)
    dq23 = after(dq23, dv_first)
    dq23 = swap(dq23, 2)
    dk1 = after(dk1, dq0)
    dk2 = after(dk2, dq0)
    stay, give = total(total_pairs_kernel, (pair, pair), dk_own, dk1, dk2)
    got = swap(give, 1)
    joined = call(join_kernel, "join", pair)(after(stay, late), got)
    crossed = swap(joined, 2)
    dv[0] = after(dv[0], joined)
    grad_value = unpack(unpack_kernel, *dv)
    dq23 = after(dq23, got)
    grad_query = unpack(unpack_turned_kernel, dq0, swap(dq1, 1), dq23, swap(dq23, 1))
    grad_key = unpack(unpack_joined_kernel, stay, got, crossed)
    passed = after(passed, grad_key)
    handoff = unpack(unpack_passed_kernel, passed)
    return (grad_query, grad_key, grad_value, handoff)


def solution(mesh):
    wide = P("section", "ctx", None)
    return jax.shard_map(
        shards,
        mesh=mesh,
        in_specs=(wide, wide, wide, wide, P("ctx", None)),
        out_specs=(wide,) * 4,
        check_vma=False,
    )
```
